128 devices in a mesh: fsdp: 8 (over y, core), ctx: 4 (over x), tp: 4 (over z).
Axes of the slice: x: 4, y: 4, z: 4, core: 2. Of those that a mesh axis runs over, the one named last changes fastest.
Arguments:
- tokens: bfloat16 [16, 1024, 2048], P('fsdp', 'ctx', 'tp'), may hold values from -6 to 6
- segments: int32 [16, 1024], P('fsdp'), may hold values from 0 to 2, as said below
- layernorm_gain: float32 [2048], P('tp'), may hold values from 0.5 to 1.5
- layernorm_bias: float32 [2048], P('tp'), may hold values from -3 to 3
- w_qkv: bfloat16 [2048, 6144], P('fsdp', 'tp'), may hold values from -0.125 to 0.125
- b_qkv: float32 [6144], P('tp'), may hold values from -4 to 4
- w_dense: bfloat16 [2048, 2048], P('fsdp', 'tp'), may hold values from -0.5 to 0.5
- b_dense: float32 [2048], P('tp'), may hold values from -4 to 4
- w_fc1: bfloat16 [2048, 8192], P('fsdp', 'tp'), may hold values from -1 to 1
- b_fc1: float32 [8192], P('tp'), may hold values from -6 to 6
- w_fc2: bfloat16 [2048, 8192], P('fsdp', 'tp'), may hold values from -0.0625 to 0.0625
- b_fc2: float32 [2048], P('tp'), may hold values from -4 to 4
- cotangent: bfloat16 [16, 1024, 2048], P('fsdp', 'ctx', 'tp'), may hold values from -6 to 6
Outputs:
- mixed: bfloat16 [16, 1024, 2048], P('fsdp', 'ctx', 'tp')
- grad_tokens: float32 [16, 1024, 2048], P('fsdp', 'ctx', 'tp')
- grad_ln_gain: float32 [2048], P('tp')
- grad_ln_bias: float32 [2048], P('tp')
- grad_w_qkv: float32 [2048, 6144], P(('fsdp', 'ctx'), 'tp')
- grad_b_qkv: float32 [6144], P('tp')
- grad_w_dense: float32 [2048, 2048], P(('fsdp', 'ctx'), 'tp')
- grad_b_dense: float32 [2048], P('tp')
- grad_w_fc1: float32 [2048, 8192], P(('fsdp', 'ctx'), 'tp')
- grad_b_fc1: float32 [8192], P('tp')
- grad_w_fc2: float32 [2048, 8192], P(('fsdp', 'ctx'), 'tp')
- grad_b_fc2: float32 [2048], P('tp')
The draws below stay inside these ranges and needn't reach their ends.
Inputs may be any that keep to these rules, and one draw needn't show every extreme that they name: `segments`: each sequence holds exactly three documents, numbered 0, 1, 2 in order; document 1 begins at a position from 1 to 127 and document 2 begins within the last 128 positions.
All inputs are finite; a program needn't handle non-finite values.
Results may differ from the reference program's by a relative error of at most 0.015.
Values may be sent and summed in bfloat16 or wider, within the bound.
No kernel may reach another device: no remote copies, remote signals or barrier semaphores. Data moves between devices by JAX's collectives and lax.ppermute only.
A program may use at most 192 MiB of HBM per device.

```python
import jax
import jax.numpy as jnp
from jax import lax

MODEL_WIDTH = 2048
H = 32
FF = 8192
ROT = 32
SEQ_LEN = 1024
SEQS = 16


def draw_segments(key, part):
    key = jax.random.fold_in(key, 11)
    first_key, last_key = jax.random.split(key, 2)
    position = jnp.arange(SEQ_LEN, dtype=jnp.int32)[None, :]
    opening = jax.random.randint(first_key, (SEQS, 1), 1, SEQ_LEN // 8)
    closing = jax.random.randint(last_key, (SEQS, 1), SEQ_LEN - SEQ_LEN // 8, SEQ_LEN)
    second = (position >= opening).astype(jnp.int32)
    third = (position >= closing).astype(jnp.int32)
    return (second + third).astype(jnp.int32)


def draw_w_fc1(key, part):
    key = jax.random.fold_in(key, 23)
    own_key, column_key = jax.random.split(key, 2)
    own = jnp.clip(jax.random.normal(own_key, (MODEL_WIDTH, FF), jnp.float32), -4.0, 4.0)
    column = jnp.clip(jax.random.normal(column_key, (1, FF), jnp.float32), -4.0, 4.0)
    return (own * MODEL_WIDTH ** (-0.5) + column * FF ** (-0.5)).astype(jnp.bfloat16)


def block_scale(stream_key, dims, cuts, low, largest):
    loudness = 1.0
    for dim, parts in cuts:
        draws = jax.random.uniform(jax.random.fold_in(jax.random.fold_in(stream_key, 6), dim), (parts,), jnp.float32, low / len(cuts), largest / len(cuts))
        loudness = loudness * jnp.repeat(jnp.exp(draws), dims[dim] // parts).reshape((-1,) + (1,) * (len(dims) - 1 - dim))
    return loudness


def bell_draw(key, extent, width, most, shards=(), held_as=jnp.bfloat16):
    entries = jax.random.normal(key, extent, jnp.float32) * width
    if len(shards) > 0:
        entries = block_scale(key, extent, shards, -0.22, 0.18) * entries
    return jnp.clip(entries, min=-most, max=most).astype(held_as)


def setup_inputs(seed: int = 0) -> dict:
    seeds = jax.random.split(jax.random.key(seed), 14)
    tokens = bell_draw(seeds[0], (SEQS, SEQ_LEN, MODEL_WIDTH), 1.0, 6.0, ((0, 8), (1, 4), (2, 4)))
    segments = draw_segments(jax.random.fold_in(seeds[13], 71), 0)
    layernorm_gain = jnp.clip(1.0 + 0.1 * jax.random.normal(seeds[2], (MODEL_WIDTH,), jnp.float32), 0.5, 1.5)
    layernorm_bias = bell_draw(seeds[3], (MODEL_WIDTH,), 0.2, 3.0, ((0, 4),), jnp.float32)
    w_qkv = bell_draw(seeds[4], (MODEL_WIDTH, 3 * MODEL_WIDTH), MODEL_WIDTH ** -0.5, 0.125, ((0, 8), (1, 4)))
    b_qkv = bell_draw(seeds[5], (3 * MODEL_WIDTH,), 0.3, 4.0, ((0, 4),), jnp.float32)
    w_dense = bell_draw(seeds[6], (MODEL_WIDTH, MODEL_WIDTH), (MODEL_WIDTH // 16) ** -0.5, 0.5, ((0, 8), (1, 4)))
    b_dense = bell_draw(seeds[7], (MODEL_WIDTH,), 0.3, 4.0, ((0, 4),), jnp.float32)
    w_fc1 = draw_w_fc1(jax.random.fold_in(seeds[13], 71), 0)
    b_fc1 = bell_draw(seeds[9], (FF,), 0.5, 6.0, ((0, 4),), jnp.float32)
    w_fc2 = bell_draw(seeds[10], (MODEL_WIDTH, FF), FF ** -0.5, 0.0625, ((0, 8), (1, 4)))
    b_fc2 = bell_draw(seeds[11], (MODEL_WIDTH,), 0.3, 4.0, ((0, 4),), jnp.float32)
    cotangent = bell_draw(seeds[12], (SEQS, SEQ_LEN, MODEL_WIDTH), 1.0, 6.0, ((0, 8), (1, 4), (2, 4)))
    return {"tokens": tokens, "segments": segments, "layernorm_gain": layernorm_gain, "layernorm_bias": layernorm_bias, "w_qkv": w_qkv, "b_qkv": b_qkv, "w_dense": w_dense, "b_dense": b_dense, "w_fc1": w_fc1, "b_fc1": b_fc1, "w_fc2": w_fc2, "b_fc2": b_fc2, "cotangent": cotangent}


@jax.custom_vjp
def low(v):
    return lax.optimization_barrier(v.astype(jnp.bfloat16)).astype(jnp.float32)

@jax.custom_vjp
def low_back(v):
    return v

def low_keep(v):
    return (low(v), None)

def low_pass(kept, grad):
    return (grad,)

def back_keep(v):
    return (v, None)

def back_low(kept, grad):
    return (low(grad),)
low.defvjp(low_keep, low_pass)
low_back.defvjp(back_keep, back_low)
EPSILON = 1e-05
MASKED = -1000000000.0

def positions_of(segments):
    length = segments.shape[-1]
    position = jnp.arange(length, dtype=jnp.int32)
    head_flag = jnp.ones(segments.shape[:-1] + (1,), dtype=jnp.bool_)
    starts_here = jnp.concatenate([head_flag, segments[..., 1:] != segments[..., :-1]], axis=-1)
    opening = lax.cummax(jnp.where(starts_here, position, 0), axis=segments.ndim - 1)
    return position - opening

def rotary_tables(positions):
    half_rot = ROT // 2
    exponent = jnp.arange(half_rot, dtype=jnp.float32) * (2.0 / ROT)
    frequency = jnp.power(10000.0, -exponent)
    angles = positions.astype(jnp.float32)[..., None] * frequency
    return (jnp.cos(angles)[..., None, :], jnp.sin(angles)[..., None, :])

def rotate(field, cosine, sine):
    half_rot = ROT // 2
    first_half = field[..., :half_rot]
    second_half = field[..., half_rot:ROT]
    return jnp.concatenate([first_half * cosine - second_half * sine, second_half * cosine + first_half * sine, field[..., ROT:]], axis=-1)

def attend_sequence(qkv_seq, segment_row):
    length = segment_row.shape[0]
    block_rows = min(512, length)
    factor = (MODEL_WIDTH // H) ** (-0.5)
    cosine, sine = rotary_tables(positions_of(segment_row))
    query = low(rotate(qkv_seq[:, :, 0], cosine, sine))
    keys = low(rotate(qkv_seq[:, :, 1], cosine, sine))
    values = qkv_seq[:, :, 2]
    position = jnp.arange(length, dtype=jnp.int32)

    def one_block(offset):
        query_rows = lax.dynamic_slice_in_dim(query, offset, block_rows, 0)
        row_segments = lax.dynamic_slice_in_dim(segment_row, offset, block_rows, 0)
        row_index = offset + jnp.arange(block_rows, dtype=jnp.int32)
        raw = jnp.einsum('qhd,khd->hqk', query_rows, keys, precision=lax.Precision.HIGHEST)
        scores = low_back(raw) * factor
        allowed = (row_segments[:, None] == segment_row[None, :]) & (position[None, :] <= row_index[:, None])
        scores = jnp.where(allowed[None], scores, MASKED)
        weights = low(jax.nn.softmax(scores, axis=-1))
        return jnp.einsum('hqk,khd->qhd', weights, values, precision=lax.Precision.HIGHEST)
    offsets = jnp.arange(length // block_rows, dtype=jnp.int32) * block_rows
    blocks = lax.map(jax.checkpoint(one_block), offsets)
    return blocks.reshape(length, MODEL_WIDTH)

def attend_packed(packed):
    return attend_sequence(packed[0], packed[1])

def reference(tokens, segments, layernorm_gain, layernorm_bias, w_qkv, b_qkv, w_dense, b_dense, w_fc1, b_fc1, w_fc2, b_fc2, cotangent):

    def forward_layer(input_rows, gain, shift, qkv_weight, qkv_bias, dense_weight, dense_bias, up_weight, up_bias, down_weight, down_bias):
        mean_removed = lax.optimization_barrier(jnp.mean(input_rows, axis=-1, keepdims=True))
        centred = input_rows - mean_removed
        spread = lax.optimization_barrier(jnp.mean(centred * centred, axis=-1, keepdims=True))
        normed = low(centred * lax.rsqrt(spread + EPSILON) * gain + shift)
        mixed_qkv = low_back(low(jnp.dot(normed, qkv_weight, precision=lax.Precision.HIGHEST) + qkv_bias))
        mixed_qkv = mixed_qkv.reshape(SEQS, SEQ_LEN, H, 3, MODEL_WIDTH // H)
        context = lax.map(jax.checkpoint(attend_packed), (mixed_qkv, segments))
        context = low_back(low(context))
        hidden = low_back(jnp.dot(normed, up_weight, precision=lax.Precision.HIGHEST) + up_bias)
        active = low(jax.nn.gelu(hidden, approximate=True))
        branch = jnp.dot(context, dense_weight.T, precision=lax.Precision.HIGHEST) + jnp.dot(active, down_weight.T, precision=lax.Precision.HIGHEST)
        return input_rows + branch + dense_bias + down_bias
    output, pullback = jax.vjp(forward_layer, tokens.astype(jnp.float32), layernorm_gain, layernorm_bias, w_qkv.astype(jnp.float32), b_qkv, w_dense.astype(jnp.float32), b_dense, w_fc1.astype(jnp.float32), b_fc1, w_fc2.astype(jnp.float32), b_fc2)
    grads = pullback(cotangent.astype(jnp.float32))
    return (output.astype(jnp.bfloat16), grads[0], grads[1], grads[2], grads[3], grads[4], grads[5], grads[6], grads[7], grads[8], grads[9], grads[10])
```

```python
import jax
import jax.numpy as jnp
from jax import lax
from jax.experimental import pallas as pl
from jax.experimental.pallas import tpu as pltpu
from jax.sharding import PartitionSpec as P

WIDTH = 2048
ROT = 32
HEAD = 64
LENGTH = 1024
ROWS = 256
TOKENS = 512
EPSILON = 1e-05
MASKED = -1000000000.0
F32 = jnp.float32
BF16 = jnp.bfloat16
MEBI = 1024 * 1024


def dot(a, b):
    return lax.dot_general(a, b, (((1,), (0,)), ((), ())), preferred_element_type=F32)


def dot_nt(a, b):
    return lax.dot_general(a, b, (((1,), (1,)), ((), ())), preferred_element_type=F32)


def shift(array, axis, step):
    return lax.ppermute(array, axis, [(i, (i + step) % 4) for i in range(4)])


def params(mebi):
    return pltpu.CompilerParams(vmem_limit_bytes=mebi * MEBI)


def cost(flops, nbytes):
    return pl.CostEstimate(flops=flops, bytes_accessed=nbytes, transcendentals=0)


def lane_block(index, width):
    return pl.ds(pl.multiple_of(index * width, 128), width)


def norm_kernel(where, t0, t1, t2, t3, g0, g1, g2, g3, normed, normed_t, rows, stats):
    tokens = (t0, t1, t2, t3)
    affine = (g0, g1, g2, g3)
    total = jnp.zeros((TOKENS, 1), F32)
    for ref in tokens:
        total += jnp.sum(ref[...].astype(F32), axis=1, keepdims=True)
    mean = total * (1.0 / WIDTH)
    square = jnp.zeros((TOKENS, 1), F32)
    for ref in tokens:
        centred = ref[...].astype(F32) - mean
        square += jnp.sum(centred * centred, axis=1, keepdims=True)
    inverse = lax.rsqrt(square * (1.0 / WIDTH) + EPSILON)
    lane = lax.broadcasted_iota(jnp.int32, (TOKENS, 128), 1)
    stats[...] = jnp.where(lane == 0, mean, inverse)
    for k in range(4):
        block = lax.rem(where[0] + 4 - k, 4)
        piece = tokens[k][...]
        rows[:, lane_block(block, 512)] = piece
        scaled = (piece.astype(F32) - mean) * inverse
        out = (scaled * affine[k][0:1, :] + affine[k][1:2, :]).astype(BF16)
        normed[:, lane_block(block, 512)] = out
        normed_t[lane_block(block, 512), :] = out.T


def join_kernel(where, t0, t1, t2, t3, full, full_t):
    for k, ref in enumerate((t0, t1, t2, t3)):
        block = lax.rem(where[0] + 4 - k, 4)
        piece = ref[...]
        full[:, lane_block(block, 512)] = piece
        full_t[lane_block(block, 512), :] = piece.T


SMEM_SPEC = pl.BlockSpec(memory_space=pltpu.SMEM)
VMEM_SPEC = pl.BlockSpec(memory_space=pltpu.VMEM)


def shape(dims, dtype):
    return jax.ShapeDtypeStruct(dims, dtype)


def norm_call(where, tokens, affine):
    return pl.pallas_call(
        norm_kernel,
        out_shape=(
            shape((TOKENS, WIDTH), BF16),
            shape((WIDTH, TOKENS), BF16),
            shape((TOKENS, WIDTH), BF16),
            shape((TOKENS, 128), F32),
        ),
        in_specs=[SMEM_SPEC] + [VMEM_SPEC] * 8,
        out_specs=[VMEM_SPEC] * 4,
        compiler_params=params(32),
        cost_estimate=cost(10 * TOKENS * WIDTH, 8 * MEBI),
        name="norm",
    )(where, *tokens, *affine)


def join_call(where, pieces):
    return pl.pallas_call(
        join_kernel,
        out_shape=(shape((TOKENS, WIDTH), BF16), shape((WIDTH, TOKENS), BF16)),
        in_specs=[SMEM_SPEC] + [VMEM_SPEC] * 4,
        out_specs=[VMEM_SPEC] * 2,
        compiler_params=params(32),
        cost_estimate=cost(TOKENS * WIDTH, 6 * MEBI),
        name="join",
    )(where, *pieces)


def project_kernel(order, normed, grad, weight, bias, *outs):
    step = pl.program_id(0)
    qkv = dot(normed[...], weight[:, :384]) + bias[...]
    context = dot(grad[...], weight[:, 384:])
    both = jnp.concatenate([qkv.astype(BF16), context.astype(BF16)], axis=1)
    for k, ref in enumerate(outs):

        @pl.when(step == k)
        def _(ref=ref):
            ref[...] = both


def project_call(order, normed, grad, weight, bias):
    count = order.shape[0]
    whole = lambda i, order: (0, 0)
    return pl.pallas_call(
        project_kernel,
        grid_spec=pltpu.PrefetchScalarGridSpec(
            num_scalar_prefetch=1,
            grid=(count,),
            in_specs=[
                pl.BlockSpec((TOKENS, WIDTH), whole),
                pl.BlockSpec((TOKENS, WIDTH), whole),
                pl.BlockSpec((WIDTH, 512), lambda i, order: (0, order[i])),
                pl.BlockSpec((1, 384), lambda i, order: (0, order[i])),
            ],
            out_specs=[pl.BlockSpec((TOKENS, 512), whole)] * count,
        ),
        out_shape=[shape((TOKENS, 512), BF16)] * count,
        compiler_params=params(40),
        cost_estimate=cost(2 * TOKENS * WIDTH * 512 * count, (4 + 2 * count) * MEBI),
        name="project",
    )(order, normed, grad, weight, bias)


def half_swap(u, lane):
    return jnp.where((lane & 31) < 16, pltpu.roll(u, 112, 1), pltpu.roll(u, 16, 1))


def attention_kernel(where, a0, a1, a2, a3, low, cosine, sine, o0, o1, o2, o3, slab, slab_t, masked, turned, grad_k, grad_v):
    lane = lax.broadcasted_iota(jnp.int32, (ROWS, 128), 1)
    left = lane < HEAD
    for k, ref in enumerate((a0, a1, a2, a3)):
        block = lax.rem(where[0] + 4 - k, 4)
        place = pl.ds(pl.multiple_of(block * ROWS, ROWS), ROWS)
        c = cosine[0, place, :]
        s = sine[0, place, :]
        u = ref[0, :, 0:128].astype(F32)
        rotated = u * c + half_swap(u, lane) * s
        first = jnp.where(left, rotated * 0.125, rotated).astype(BF16)
        u = ref[0, :, 128:256].astype(F32)
        rotated = u * c + half_swap(u, lane) * s
        second = jnp.where(left, u, rotated * 0.125).astype(BF16)
        u = ref[0, :, 256:384].astype(F32)
        rotated = u * c + half_swap(u, lane) * s
        third = jnp.where(left, rotated, u).astype(BF16)
        fourth = ref[0, :, 384:512]
        slab[place, 0:128] = first
        slab[place, 128:256] = second
        slab[place, 256:384] = third
        slab[place, 384:512] = fourth
        zero = jnp.zeros((ROWS, 128), BF16)
        masked[place, 0:128] = jnp.where(left, first, zero)
        masked[place, 128:256] = jnp.where(left, zero, second)
        masked[place, 256:384] = jnp.where(left, fourth, zero)
        masked[place, 384:512] = jnp.where(left, zero, fourth)
    for i in range(4):
        place = slice(i * ROWS, (i + 1) * ROWS)
        for j in range(4):
            slab_t[j * 128 : (j + 1) * 128, place] = slab[place, j * 128 : (j + 1) * 128].T
    zeros = jnp.zeros((HEAD, ROWS), BF16)
    for i in range(4):
        own = slice(i * ROWS, (i + 1) * ROWS)
        end = (i + 1) * ROWS
        start = low[0, 0:1, own]
        key = lax.broadcasted_iota(jnp.int32, (ROWS, ROWS), 0)
        query = lax.broadcasted_iota(jnp.int32, (ROWS, ROWS), 1)
        causal = key <= query
        for h in range(2):
            if h == 0:
                keys = slab[0:end, 0:128]
                values = slab[0:end, 128:256]
                query_t = jnp.concatenate([zeros, slab_t[0:64, own]], axis=0)
                grad_t = jnp.concatenate([slab_t[384:448, own], zeros], axis=0)
                key_rows, value_rows = slice(64, 128), slice(128, 192)
            else:
                keys = slab[0:end, 256:384]
                values = slab[0:end, 256:384]
                query_t = jnp.concatenate([slab_t[192:256, own], zeros], axis=0)
                grad_t = jnp.concatenate([zeros, slab_t[448:512, own]], axis=0)
                key_rows, value_rows = slice(256, 320), slice(320, 384)
            score = dot(keys, query_t)
            pieces = []
            for j in range(i + 1):
                piece = score[j * ROWS : (j + 1) * ROWS]
                allowed = None
                if j == 0 or i == 3:
                    allowed = key + j * ROWS >= start
                if j == i:
                    allowed = causal if allowed is None else allowed & causal
                if allowed is not None:
                    piece = jnp.where(allowed, piece, MASKED)
                pieces.append(piece)
            score = jnp.concatenate(pieces, axis=0) if len(pieces) > 1 else pieces[0]
            largest = jnp.max(score, axis=0, keepdims=True)
            weight = jnp.exp(score - largest)
            total = jnp.sum(weight, axis=0, keepdims=True)
            weight = weight * (1.0 / total)
            rounded = weight.astype(BF16)
            grad_weight = dot(values, grad_t)
            inner = jnp.sum(weight * grad_weight, axis=0, keepdims=True)
            grad_score = (weight * (grad_weight - inner)).astype(BF16)
            turned[h * 64 : h * 64 + 64, own] = dot(slab_t[key_rows, 0:end], grad_score)
            turned[128 + h * 64 : 192 + h * 64, own] = dot(slab_t[value_rows, 0:end], rounded)
            add_k = dot(grad_score, masked[own, h * 128 : (h + 1) * 128])
            add_v = dot(rounded, masked[own, 256 + h * 128 : 384 + h * 128])
            if h == 0:
                new_k, new_v = add_k, add_v
            else:
                new_k, new_v = new_k + add_k, new_v + add_v
        if i > 0:
            before = slice(0, i * ROWS)
            grad_k[before, :] += new_k[0 : i * ROWS]
            grad_v[before, :] += new_v[0 : i * ROWS]
        grad_k[own, :] = new_k[i * ROWS :]
        grad_v[own, :] = new_v[i * ROWS :]
    for k, ref in enumerate((o0, o1, o2, o3)):
        block = lax.rem(where[0] + 4 - k, 4)
        place = pl.ds(pl.multiple_of(block * ROWS, ROWS), ROWS)
        c = cosine[0, place, :]
        s = sine[0, place, :]
        gq = turned[0:128, place].T * 0.125
        gq = gq * c - half_swap(gq, lane) * s
        gk = grad_k[place, :]
        gk = gk * c - half_swap(gk, lane) * s
        gv = grad_v[place, :]
        gk = pltpu.roll(gk, 64, 1)
        ref[0, :, 0:128] = jnp.where(left, gq, gk).astype(BF16)
        ref[0, :, 128:256] = jnp.where(left, gv, gq).astype(BF16)
        ref[0, :, 256:384] = jnp.where(left, gk, gv).astype(BF16)
        ref[0, :, 384:512] = turned[128:256, place].T.astype(BF16)


def attention_call(where, pieces, low, cosine, sine):
    seqs = low.shape[0]
    row = lambda i: (i, 0, 0)
    block = pl.BlockSpec((1, ROWS, 512), row)
    return pl.pallas_call(
        attention_kernel,
        grid=(seqs,),
        in_specs=[SMEM_SPEC]
        + [block] * 4
        + [
            pl.BlockSpec((1, 8, LENGTH), row),
            pl.BlockSpec((1, LENGTH, 128), row),
            pl.BlockSpec((1, LENGTH, 128), row),
        ],
        out_specs=[block] * 4,
        out_shape=[shape((seqs, ROWS, 512), BF16)] * 4,
        scratch_shapes=[
            pltpu.VMEM((LENGTH, 512), BF16),
            pltpu.VMEM((512, LENGTH), BF16),
            pltpu.VMEM((LENGTH, 512), BF16),
            pltpu.VMEM((256, LENGTH), F32),
            pltpu.VMEM((LENGTH, 128), F32),
            pltpu.VMEM((LENGTH, 128), F32),
        ],
        compiler_params=params(48),
        cost_estimate=cost(16 * 1000 * 1000 * 1000, 12 * MEBI),
        name="attention",
    )(where, *pieces, low, cosine, sine)


def mlp_kernel(normed, normed_t, grad, grad_t, up, down, bias, weight_grad, branch, back, bias_grad):
    step = pl.program_id(0)
    hidden = dot(normed[...], up[...]) + bias[...]
    square = hidden * hidden
    slope = 0.7978845608028654
    turn = jnp.tanh(slope * (hidden + 0.044715 * (square * hidden)))
    half = 0.5 * (1.0 + turn)
    active = (hidden * half).astype(BF16)
    derivative = half + 0.5 * hidden * (1.0 - turn * turn) * (slope * (1.0 + 0.134145 * square))
    grad_hidden = (dot(grad[...], down[...]) * derivative).astype(BF16)
    weight_grad[0] = dot(normed_t[...], grad_hidden).astype(BF16)
    weight_grad[1] = dot(grad_t[...], active).astype(BF16)
    bias_grad[...] = jnp.sum(grad_hidden.astype(F32), axis=0, keepdims=True)
    add_branch = dot_nt(active, down[...])
    add_back = dot_nt(grad_hidden, up[...])

    @pl.when(step == 0)
    def _():
        branch[...] = add_branch
        back[...] = add_back

    @pl.when(step > 0)
    def _():
        branch[...] += add_branch
        back[...] += add_back


def mlp_call(normed, normed_t, grad, grad_t, weight, bias):
    half = weight.shape[1] // 2
    steps = half // 256
    whole = lambda i: (0, 0)
    once = pl.Buffered(1)
    return pl.pallas_call(
        mlp_kernel,
        grid=(steps,),
        in_specs=[
            pl.BlockSpec((TOKENS, WIDTH), whole, pipeline_mode=once),
            pl.BlockSpec((WIDTH, TOKENS), whole, pipeline_mode=once),
            pl.BlockSpec((TOKENS, WIDTH), whole, pipeline_mode=once),
            pl.BlockSpec((WIDTH, TOKENS), whole, pipeline_mode=once),
            pl.BlockSpec((WIDTH, 256), lambda i: (0, i)),
            pl.BlockSpec((WIDTH, 256), lambda i: (0, i + steps)),
            pl.BlockSpec((1, 256), lambda i: (0, i)),
        ],
        out_specs=[
            pl.BlockSpec((2, WIDTH, 256), lambda i: (0, 0, i)),
            pl.BlockSpec((TOKENS, WIDTH), whole),
            pl.BlockSpec((TOKENS, WIDTH), whole),
            pl.BlockSpec((1, 256), lambda i: (0, i)),
        ],
        out_shape=[
            shape((2, WIDTH, half), BF16),
            shape((TOKENS, WIDTH), F32),
            shape((TOKENS, WIDTH), F32),
            shape((1, half), F32),
        ],
        compiler_params=params(56),
        cost_estimate=cost(12 * TOKENS * WIDTH * half, 32 * MEBI),
        name="mlp",
    )(normed, normed_t, grad, grad_t, weight, weight, bias)


def post_kernel(order, q0, q1, q2, q3, normed_t, grad_t, weight, weight_grad, branch, back, bias_grad, held):
    step = pl.program_id(0)

    @pl.when(step == 0)
    def _():
        for k, ref in enumerate((q0, q1, q2, q3)):
            held[k] = ref[...]

    both = held[step]
    grad_qkv = both[:, :384]
    context = both[:, 384:]
    weight_grad[:, :384] = dot(normed_t[...], grad_qkv).astype(BF16)
    weight_grad[:, 384:] = dot(grad_t[...], context).astype(BF16)
    bias_grad[...] = jnp.sum(grad_qkv.astype(F32), axis=0, keepdims=True)
    add_back = dot_nt(grad_qkv, weight[:, :384])
    add_branch = dot_nt(context, weight[:, 384:])

    @pl.when(step == 0)
    def _():
        branch[...] = add_branch
        back[...] = add_back

    @pl.when(step > 0)
    def _():
        branch[...] += add_branch
        back[...] += add_back


def post_call(order, pieces, normed_t, grad_t, weight):
    whole = lambda i, order: (0, 0)
    once = pl.Buffered(1)
    return pl.pallas_call(
        post_kernel,
        grid_spec=pltpu.PrefetchScalarGridSpec(
            num_scalar_prefetch=1,
            grid=(4,),
            in_specs=[pl.BlockSpec((TOKENS, 512), whole, pipeline_mode=once)] * 4
            + [
                pl.BlockSpec((WIDTH, TOKENS), whole, pipeline_mode=once),
                pl.BlockSpec((WIDTH, TOKENS), whole, pipeline_mode=once),
                pl.BlockSpec((WIDTH, 512), lambda i, order: (0, order[i])),
            ],
            out_specs=[
                pl.BlockSpec((WIDTH, 512), lambda i, order: (0, order[i])),
                pl.BlockSpec((TOKENS, WIDTH), whole),
                pl.BlockSpec((TOKENS, WIDTH), whole),
                pl.BlockSpec((1, 384), lambda i, order: (0, order[i])),
            ],
            scratch_shapes=[pltpu.VMEM((4, TOKENS, 512), BF16)],
        ),
        out_shape=[
            shape((WIDTH, WIDTH), BF16),
            shape((TOKENS, WIDTH), F32),
            shape((TOKENS, WIDTH), F32),
            shape((1, 1536), F32),
        ],
        compiler_params=params(56),
        cost_estimate=cost(4 * TOKENS * WIDTH * WIDTH, 32 * MEBI),
        name="post",
    )(order, *pieces, normed_t, grad_t, weight)


def split_two(value):
    high = value.astype(BF16)
    return high, (value - high.astype(F32)).astype(BF16)


def finish_kernel(where, b0, b1, b2, g0, g1, g2, rows, stats, gain, m0, m1, m2, m3, u0, u1, u2, u3):
    mean = stats[:, 0:1]
    inverse = stats[:, 1:2]
    first = jnp.zeros((TOKENS, 1), F32)
    second = jnp.zeros((TOKENS, 1), F32)
    for j in range(4):
        part = slice(j * 512, (j + 1) * 512)
        scaled = (g0[:, part] + g1[:, part] + g2[:, part]) * gain[0:1, part]
        standard = (rows[:, part].astype(F32) - mean) * inverse
        first += jnp.sum(scaled, axis=1, keepdims=True)
        second += jnp.sum(scaled * standard, axis=1, keepdims=True)
    first = first * (1.0 / WIDTH)
    second = second * (1.0 / WIDTH)
    for k, (mix, out) in enumerate(((m0, u0), (m1, u1), (m2, u2), (m3, u3))):
        part = lane_block(lax.rem(where[0] + k, 4), 512)
        mix[...] = (b0[:, part] + b1[:, part] + b2[:, part]).astype(BF16)
        raw = g0[:, part] + g1[:, part] + g2[:, part]
        standard = (rows[:, part].astype(F32) - mean) * inverse
        out[0:TOKENS, :] = (inverse * (raw * gain[0:1, part] - first - standard * second)).astype(BF16)
        high_gain, low_gain = split_two(jnp.sum(raw * standard, axis=0, keepdims=True))
        high_shift, low_shift = split_two(jnp.sum(raw, axis=0, keepdims=True))
        row = lax.broadcasted_iota(jnp.int32, (16, 512), 0)
        tail = jnp.where(row == 0, high_gain, jnp.where(row == 1, low_gain, jnp.where(row == 2, high_shift, low_shift)))
        out[TOKENS : TOKENS + 16, :] = tail


def finish_call(where, branches, backs, rows, stats, gain):
    return pl.pallas_call(
        finish_kernel,
        out_shape=[shape((TOKENS, 512), BF16)] * 4 + [shape((TOKENS + 16, 512), BF16)] * 4,
        in_specs=[SMEM_SPEC] + [VMEM_SPEC] * 9,
        out_specs=[VMEM_SPEC] * 8,
        compiler_params=params(56),
        cost_estimate=cost(20 * TOKENS * WIDTH, 32 * MEBI),
        name="finish",
    )(where, *branches, *backs, rows, stats, gain)


def exchange_sum(value):
    for bit in (1, 2, 4):
        value = value + lax.ppermute(value, "fsdp", [(i, i ^ bit) for i in range(8)])
    for bit in (1, 2):
        value = value + lax.ppermute(value, "ctx", [(i, i ^ bit) for i in range(4)])
    return value


def rotary_tables(segments):
    position = jnp.arange(LENGTH, dtype=jnp.int32)[None, :]
    one = jnp.sum((segments < 1).astype(jnp.int32), axis=1, keepdims=True)
    two = jnp.sum((segments < 2).astype(jnp.int32), axis=1, keepdims=True)
    low = jnp.where(segments == 0, 0, jnp.where(segments == 1, one, two))
    exponent = jnp.arange(ROT // 2, dtype=F32) * (2.0 / ROT)
    frequency = jnp.power(10000.0, -exponent)
    angles = (position - low).astype(F32)[..., None] * frequency
    c, s = jnp.cos(angles), jnp.sin(angles)
    keep = jnp.ones(c.shape[:2] + (32,), F32)
    cosine = jnp.concatenate([c, c, keep, c, c, keep], axis=-1)
    sine = jnp.concatenate([-s, s, 0.0 * keep, -s, s, 0.0 * keep], axis=-1)
    return jnp.broadcast_to(low[:, None, :], (low.shape[0], 8, LENGTH)), cosine, sine


def local(tokens, segments, gain, shift_, w_qkv, b_qkv, w_dense, b_dense, w_fc1, b_fc1, w_fc2, b_fc2, cotangent):
    x = lax.axis_index("ctx").astype(jnp.int32)
    z = lax.axis_index("tp").astype(jnp.int32)
    seqs = tokens.shape[0]
    mine = tokens.reshape(TOKENS, 512)
    grad = cotangent.reshape(TOKENS, 512)
    where_x, where_z = x[None], z[None]

    attention_part = jnp.concatenate(
        [w[:, k * n : (k + 1) * n] for k in range(4) for w, n in ((w_qkv, 384), (w_dense, 128))], axis=1
    )
    wa = lax.all_gather(attention_part, "fsdp", axis=0, tiled=True)
    wf = []
    for j in range(2):
        cut = slice(j * 1024, (j + 1) * 1024)
        part = jnp.concatenate([w_fc1[:, cut], w_fc2[:, cut]], axis=1)
        wf.append(lax.all_gather(part, "fsdp", axis=0, tiled=True))

    affine = jnp.stack([gain, shift_])
    affines = [affine] + [shift(affine, "tp", k) for k in (1, 2, 3)]
    token_pieces = [mine] + [shift(mine, "tp", k) for k in (1, 2, 3)]
    grad_pieces = [grad] + [shift(grad, "tp", k) for k in (1, 2, 3)]
    normed, normed_t, rows, stats = norm_call(where_z, token_pieces, affines)
    grad_full, grad_t = join_call(where_z, grad_pieces)
    order_z = (z + 4 - jnp.arange(4, dtype=jnp.int32)) % 4
    gain_full = jnp.zeros((4, 512), F32)
    for k in range(4):
        gain_full = lax.dynamic_update_slice(gain_full, affines[k][0:1], (order_z[k], 0))
    gain_full = gain_full.reshape(1, WIDTH)

    order = (x + jnp.arange(4, dtype=jnp.int32)) % 4
    bias = b_qkv.reshape(1, 1536)
    sent = project_call(order[1:], normed, grad_full, wa, bias)
    kept = project_call(order[:1], normed, grad_full, wa, bias)
    arrived = [kept[0]] + [shift(a, "ctx", k + 1) for k, a in enumerate(sent)]
    low, cosine, sine = rotary_tables(segments)
    done = attention_call(where_x, [a.reshape(seqs, ROWS, 512) for a in arrived], low, cosine, sine)
    done = [a.reshape(TOKENS, 512) for a in done]
    returned = [done[0]] + [shift(a, "ctx", 4 - k) for k, a in enumerate(done) if k > 0]

    ff = [
        mlp_call(normed, normed_t, grad_full, grad_t, wf[j], b_fc1[j * 1024 : (j + 1) * 1024].reshape(1, 1024))
        for j in range(2)
    ]
    post = post_call(order, returned, normed_t, grad_t, wa)
    pieces = finish_call(
        where_z,
        [post[1], ff[0][1], ff[1][1]],
        [post[2], ff[0][2], ff[1][2]],
        rows,
        stats,
        gain_full,
    )
    mixes = [pieces[0]] + [shift(pieces[k], "tp", k) for k in (1, 2, 3)]
    backs = [pieces[4]] + [shift(pieces[4 + k], "tp", k) for k in (1, 2, 3)]
    branch = sum(m.astype(F32) for m in mixes)
    mixed = (mine.astype(F32) + branch + b_dense + b_fc2).astype(BF16).reshape(tokens.shape)
    back = sum(m[:TOKENS].astype(F32) for m in backs)
    grad_tokens = (grad.astype(F32) + back).reshape(tokens.shape)
    tails = sum(m[TOKENS : TOKENS + 4].astype(F32) for m in backs)

    def scatter(value, dim):
        value = lax.psum_scatter(value, "fsdp", scatter_dimension=dim, tiled=True)
        return lax.psum_scatter(value, "ctx", scatter_dimension=dim, tiled=True).astype(F32)

    ga = scatter(post[0], 0).reshape(64, 4, 512)
    grad_w_qkv = ga[:, :, :384].reshape(64, 1536)
    grad_w_dense = ga[:, :, 384:].reshape(64, 512)
    gf = [scatter(f[0], 1) for f in ff]
    grad_w_fc1 = jnp.concatenate([gf[0][0], gf[1][0]], axis=1)
    grad_w_fc2 = jnp.concatenate([gf[0][1], gf[1][1]], axis=1)

    small = jnp.concatenate(
        [
            tails[0] + tails[1],
            tails[2] + tails[3],
            jnp.sum(grad.astype(F32), axis=0),
            post[3][0],
            ff[0][3][0],
            ff[1][3][0],
        ]
    )
    small = exchange_sum(small)
    grad_b_out = small[1024:1536]
    return (
        mixed,
        grad_tokens,
        small[:512],
        small[512:1024],
        grad_w_qkv,
        small[1536:3072],
        grad_w_dense,
        grad_b_out,
        grad_w_fc1,
        small[3072:],
        grad_w_fc2,
        grad_b_out,
    )


def solution(mesh):
    token = P("fsdp", "ctx", "tp")
    weight = P("fsdp", "tp")
    weight_grad = P(("fsdp", "ctx"), "tp")
    vector = P("tp")
    return jax.shard_map(
        local,
        mesh=mesh,
        in_specs=(
            token, P("fsdp", None), vector, vector, weight, vector, weight, vector, weight, vector, weight, vector, token,
        ),
        out_specs=(
            token, token, vector, vector, weight_grad, vector, weight_grad, vector, weight_grad, vector, weight_grad, vector,
        ),
        check_vma=False,
    )
```

```python
import jax
import jax.numpy as jnp
from jax import lax
from jax.experimental import pallas as pl
from jax.experimental.pallas import tpu as pltpu
from jax.sharding import PartitionSpec as P

WIDTH = 2048
ROT = 32
HEAD = 64
LENGTH = 1024
ROWS = 256
TOKENS = 512
EPSILON = 1e-05
MASKED = -1000000000.0
F32 = jnp.float32
BF16 = jnp.bfloat16
MEBI = 1024 * 1024


def dot(a, b):
    return lax.dot_general(a, b, (((1,), (0,)), ((), ())), preferred_element_type=F32)


def dot_nt(a, b):
    return lax.dot_general(a, b, (((1,), (1,)), ((), ())), preferred_element_type=F32)


def shift(array, axis, step):
    return lax.ppermute(array, axis, [(i, (i + step) % 4) for i in range(4)])


def params(mebi):
    return pltpu.CompilerParams(vmem_limit_bytes=mebi * MEBI)


def cost(microseconds):
    return pl.CostEstimate(flops=int(microseconds * 1.15e9), bytes_accessed=1024, transcendentals=0)


def lane_block(index, width):
    return pl.ds(pl.multiple_of(index * width, 128), width)


def place_rows(where, block, piece, natural, sorted_):
    turned = piece.T
    natural[lane_block(block, 512), :] = turned
    for core in range(2):
        for column in range(4):
            to_core = 1 - (where[3] ^ core)
            to_x = lax.rem(column + 4 - where[1], 4)
            to_y = lax.rem(block + 4 - where[2], 4)
            row = ((to_core * 4 + to_x) * 4 + to_y) * 64
            first = (core * 4 + column) * 64
            sorted_[pl.ds(pl.multiple_of(row, 64), 64), :] = turned[first : first + 64]


def norm_kernel(where, t0, t1, t2, t3, normed, natural, sorted_, rows, stats, gains):
    tokens = (t0, t1, t2, t3)
    total = jnp.zeros((TOKENS, 1), F32)
    for ref in tokens:
        total += jnp.sum(ref[:TOKENS, :].astype(F32), axis=1, keepdims=True)
    mean = total * (1.0 / WIDTH)
    square = jnp.zeros((TOKENS, 1), F32)
    for ref in tokens:
        centred = ref[:TOKENS, :].astype(F32) - mean
        square += jnp.sum(centred * centred, axis=1, keepdims=True)
    inverse = lax.rsqrt(square * (1.0 / WIDTH) + EPSILON)
    lane = lax.broadcasted_iota(jnp.int32, (TOKENS, 128), 1)
    stats[...] = jnp.where(lane == 0, mean, inverse)
    for k, ref in enumerate(tokens):
        block = lax.rem(where[0] + 4 - k, 4)
        affine = ref[TOKENS:, :].astype(F32)
        gain = (affine[0:1] + affine[1:2]) + affine[2:3]
        bias = (affine[3:4] + affine[4:5]) + affine[5:6]
        gains[block] = gain
        piece = ref[:TOKENS, :]
        rows[:, lane_block(block, 512)] = piece
        scaled = (piece.astype(F32) - mean) * inverse
        out = (scaled * gain + bias).astype(BF16)
        normed[:, lane_block(block, 512)] = out
        place_rows(where, block, out, natural, sorted_)


def join_kernel(where, t0, t1, t2, t3, full, natural, sorted_):
    for k, ref in enumerate((t0, t1, t2, t3)):
        block = lax.rem(where[0] + 4 - k, 4)
        piece = ref[...]
        full[:, lane_block(block, 512)] = piece
        place_rows(where, block, piece, natural, sorted_)


ONCE = pl.Buffered(1)
SMEM_SPEC = pl.BlockSpec(memory_space=pltpu.SMEM)
VMEM_SPEC = pl.BlockSpec(memory_space=pltpu.VMEM)


def shape(dims, dtype):
    return jax.ShapeDtypeStruct(dims, dtype)


def split_three(value):
    parts = []
    for _ in range(3):
        part = lax.reduce_precision(value, exponent_bits=8, mantissa_bits=7)
        parts.append(part.astype(BF16))
        value = value - part
    return parts


def norm_call(where, tokens):
    return pl.pallas_call(
        norm_kernel,
        out_shape=(
            shape((TOKENS, WIDTH), BF16),
            shape((WIDTH, TOKENS), BF16),
            shape((WIDTH, TOKENS), BF16),
            shape((TOKENS, WIDTH), BF16),
            shape((TOKENS, 128), F32),
            shape((4, 1, 512), F32),
        ),
        in_specs=[SMEM_SPEC] + [VMEM_SPEC] * 4,
        out_specs=[VMEM_SPEC] * 6,
        compiler_params=params(60),
        cost_estimate=cost(7),
        name="norm",
    )(where, *tokens)


def join_call(where, pieces):
    return pl.pallas_call(
        join_kernel,
        out_shape=(shape((TOKENS, WIDTH), BF16), shape((WIDTH, TOKENS), BF16), shape((WIDTH, TOKENS), BF16)),
        in_specs=[SMEM_SPEC] + [VMEM_SPEC] * 4,
        out_specs=[VMEM_SPEC] * 3,
        compiler_params=params(60),
        cost_estimate=cost(5),
        name="join",
    )(where, *pieces)


def pick_kernel(where, w_qkv, w_dense, w_fc1, w_fc2, out):
    out[:, 0:1536] = w_qkv[...]
    out[:, 1536:2048] = w_dense[...]
    out[:, 2048:3072] = w_fc1[...]
    out[:, 3072:4096] = w_fc2[...]


def pick_call(x, w_qkv, w_dense, w_fc1, w_fc2):
    here = lambda i, x: (x[0], 0)
    return pl.pallas_call(
        pick_kernel,
        grid_spec=pltpu.PrefetchScalarGridSpec(
            num_scalar_prefetch=1,
            grid=(1,),
            in_specs=[pl.BlockSpec((64, n), here) for n in (1536, 512, 1024, 1024)],
            out_specs=pl.BlockSpec((64, 4096), lambda i, x: (0, 0)),
        ),
        out_shape=shape((64, 4096), BF16),
        compiler_params=params(60),
        cost_estimate=cost(1),
        name="pick",
    )(x, w_qkv, w_dense, w_fc1, w_fc2)


def project_kernel(order, normed, grad, w_qkv, w_dense, bias, *outs):
    step = pl.program_id(0)
    qkv = dot(normed[...], w_qkv[...]) + bias[...]
    context = dot(grad[...], w_dense[...])
    both = jnp.concatenate([qkv.astype(BF16), context.astype(BF16)], axis=1)
    for k, ref in enumerate(outs):

        @pl.when(step == k)
        def _(ref=ref):
            ref[...] = both


def project_call(order, normed, grad, weight, bias, estimate):
    count = order.shape[0]
    whole = lambda i, order: (0, 0)
    return pl.pallas_call(
        project_kernel,
        grid_spec=pltpu.PrefetchScalarGridSpec(
            num_scalar_prefetch=1,
            grid=(count,),
            in_specs=[
                pl.BlockSpec((TOKENS, WIDTH), whole, pipeline_mode=ONCE),
                pl.BlockSpec((TOKENS, WIDTH), whole, pipeline_mode=ONCE),
                pl.BlockSpec((WIDTH, 384), lambda i, order: (0, order[i])),
                pl.BlockSpec((WIDTH, 128), lambda i, order: (0, 12 + order[i])),
                pl.BlockSpec((1, 384), lambda i, order: (0, order[i])),
            ],
            out_specs=[pl.BlockSpec((TOKENS, 512), whole)] * count,
        ),
        out_shape=[shape((TOKENS, 512), BF16)] * count,
        compiler_params=params(60),
        cost_estimate=cost(estimate),
        name="project",
    )(order, normed, grad, weight, weight, bias)


def half_swap(u, lane):
    return jnp.where((lane & 31) < 16, pltpu.roll(u, 112, 1), pltpu.roll(u, 16, 1))


def attention_kernel(where, a0, a1, a2, a3, low, narrow_c, narrow_s, o0, o1, o2, o3, slab, slab_t, masked, turned, grad_k, grad_v, cosine, sine):
    lane = lax.broadcasted_iota(jnp.int32, (ROWS, 128), 1)
    left = lane < HEAD
    for i in range(4):
        place = slice(i * ROWS, (i + 1) * ROWS)
        c = narrow_c[0, :, place]
        s = narrow_s[0, :, place]
        one = jnp.ones((32, ROWS), F32)
        cosine[place, :] = jnp.concatenate([c, c, one, c, c, one], axis=0).T
        one = jnp.zeros((32, ROWS), F32)
        sine[place, :] = jnp.concatenate([-s, s, one, -s, s, one], axis=0).T
    for k, ref in enumerate((a0, a1, a2, a3)):
        block = lax.rem(where[0] + 4 - k, 4)
        place = pl.ds(pl.multiple_of(block * ROWS, ROWS), ROWS)
        c = cosine[place, :]
        s = sine[place, :]
        u = ref[0, :, 0:128].astype(F32)
        rotated = u * c + half_swap(u, lane) * s
        first = jnp.where(left, rotated * 0.125, rotated).astype(BF16)
        u = ref[0, :, 128:256].astype(F32)
        rotated = u * c + half_swap(u, lane) * s
        second = jnp.where(left, u, rotated * 0.125).astype(BF16)
        u = ref[0, :, 256:384].astype(F32)
        rotated = u * c + half_swap(u, lane) * s
        third = jnp.where(left, rotated, u).astype(BF16)
        fourth = ref[0, :, 384:512]
        slab[place, 0:128] = first
        slab[place, 128:256] = second
        slab[place, 256:384] = third
        slab[place, 384:512] = fourth
        zero = jnp.zeros((ROWS, 128), BF16)
        masked[place, 0:128] = jnp.where(left, first, zero)
        masked[place, 128:256] = jnp.where(left, zero, second)
        masked[place, 256:384] = jnp.where(left, fourth, zero)
        masked[place, 384:512] = jnp.where(left, zero, fourth)
    for i in range(4):
        place = slice(i * ROWS, (i + 1) * ROWS)
        for j in range(4):
            slab_t[j * 128 : (j + 1) * 128, place] = slab[place, j * 128 : (j + 1) * 128].T
    zeros = jnp.zeros((HEAD, ROWS), BF16)
    for i in range(4):
        own = slice(i * ROWS, (i + 1) * ROWS)
        end = (i + 1) * ROWS
        start = low[0, 0:1, own]
        key = lax.broadcasted_iota(jnp.int32, (ROWS, ROWS), 0)
        query = lax.broadcasted_iota(jnp.int32, (ROWS, ROWS), 1)
        causal = key <= query
        for h in range(2):
            if h == 0:
                keys = slab[0:end, 0:128]
                values = slab[0:end, 128:256]
                query_t = jnp.concatenate([zeros, slab_t[0:64, own]], axis=0)
                grad_t = jnp.concatenate([slab_t[384:448, own], zeros], axis=0)
                key_rows, value_rows = slice(64, 128), slice(128, 192)
            else:
                keys = slab[0:end, 256:384]
                values = slab[0:end, 256:384]
                query_t = jnp.concatenate([slab_t[192:256, own], zeros], axis=0)
                grad_t = jnp.concatenate([zeros, slab_t[448:512, own]], axis=0)
                key_rows, value_rows = slice(256, 320), slice(320, 384)
            score = dot(keys, query_t)
            pieces = []
            for j in range(i + 1):
                piece = score[j * ROWS : (j + 1) * ROWS]
                allowed = None
                if j == 0 or i == 3:
                    allowed = key + j * ROWS >= start
                if j == i:
                    allowed = causal if allowed is None else allowed & causal
                if allowed is not None:
                    piece = jnp.where(allowed, piece, MASKED)
                pieces.append(piece)
            score = jnp.concatenate(pieces, axis=0) if len(pieces) > 1 else pieces[0]
            largest = jnp.max(score, axis=0, keepdims=True)
            weight = jnp.exp(score - largest)
            total = jnp.sum(weight, axis=0, keepdims=True)
            weight = weight * (1.0 / total)
            rounded = weight.astype(BF16)
            grad_weight = dot(values, grad_t)
            inner = jnp.sum(weight * grad_weight, axis=0, keepdims=True)
            grad_score = (weight * (grad_weight - inner)).astype(BF16)
            turned[h * 64 : h * 64 + 64, own] = dot(slab_t[key_rows, 0:end], grad_score)
            turned[128 + h * 64 : 192 + h * 64, own] = dot(slab_t[value_rows, 0:end], rounded)
            add_k = dot(grad_score, masked[own, h * 128 : (h + 1) * 128])
            add_v = dot(rounded, masked[own, 256 + h * 128 : 384 + h * 128])
            if h == 0:
                new_k, new_v = add_k, add_v
            else:
                new_k, new_v = new_k + add_k, new_v + add_v
        if i > 0:
            before = slice(0, i * ROWS)
            grad_k[before, :] += new_k[0 : i * ROWS]
            grad_v[before, :] += new_v[0 : i * ROWS]
        grad_k[own, :] = new_k[i * ROWS :]
        grad_v[own, :] = new_v[i * ROWS :]
    for k, ref in enumerate((o0, o1, o2, o3)):
        block = lax.rem(where[0] + 4 - k, 4)
        place = pl.ds(pl.multiple_of(block * ROWS, ROWS), ROWS)
        c = cosine[place, :]
        s = sine[place, :]
        gq = turned[0:128, place].T * 0.125
        gq = gq * c - half_swap(gq, lane) * s
        gk = grad_k[place, :]
        gk = gk * c - half_swap(gk, lane) * s
        gv = grad_v[place, :]
        gk = pltpu.roll(gk, 64, 1)
        ref[0, :, 0:128] = jnp.where(left, gq, gk).astype(BF16)
        ref[0, :, 128:256] = jnp.where(left, gv, gq).astype(BF16)
        ref[0, :, 256:384] = jnp.where(left, gk, gv).astype(BF16)
        ref[0, :, 384:512] = turned[128:256, place].T.astype(BF16)


def attention_call(where, pieces, low, cosine, sine):
    seqs = low.shape[0]
    row = lambda i: (i, 0, 0)
    block = pl.BlockSpec((1, ROWS, 512), row)
    return pl.pallas_call(
        attention_kernel,
        grid=(seqs,),
        in_specs=[SMEM_SPEC]
        + [block] * 4
        + [
            pl.BlockSpec((1, 8, LENGTH), row),
            pl.BlockSpec((1, 16, LENGTH), row),
            pl.BlockSpec((1, 16, LENGTH), row),
        ],
        out_specs=[block] * 4,
        out_shape=[shape((seqs, ROWS, 512), BF16)] * 4,
        scratch_shapes=[
            pltpu.VMEM((LENGTH, 512), BF16),
            pltpu.VMEM((512, LENGTH), BF16),
            pltpu.VMEM((LENGTH, 512), BF16),
            pltpu.VMEM((256, LENGTH), F32),
            pltpu.VMEM((LENGTH, 128), F32),
            pltpu.VMEM((LENGTH, 128), F32),
            pltpu.VMEM((LENGTH, 128), F32),
            pltpu.VMEM((LENGTH, 128), F32),
        ],
        compiler_params=params(60),
        cost_estimate=cost(8),
        name="attention",
    )(where, *pieces, low, cosine, sine)


def fold_kernel(forth, back, normed_t, grad_t, came, *outs):
    step = pl.program_id(0)
    first = dot(normed_t[...], back[...])
    second = dot(grad_t[...], forth[...])
    width = first.shape[1]
    if came.shape[0] == 2:
        first = (first + came[0].astype(F32)).astype(BF16)
        second = (second + came[1].astype(F32)).astype(BF16)
    else:
        first = (first + came[0, :, :width].astype(F32)).astype(BF16)
        second = (second + came[0, :, width:].astype(F32)).astype(BF16)

    def store(ref, rows):
        if ref.shape[0] == 2:
            ref[0] = first[rows]
            ref[1] = second[rows]
        else:
            ref[0, :, :width] = first[rows]
            ref[0, :, width:] = second[rows]

    place = (0, 1, 2, 3) if len(outs) == 4 else (0, 1, None, 4)
    for k in range(4):

        @pl.when(step == k)
        def _(k=k):
            if place[k] is None:
                store(outs[2], slice(0, 128))
                store(outs[3], slice(128, 256))
            else:
                store(outs[place[k]], slice(0, 256))


def fold_call(forth, back, normed_t, grad_t, came, sizes, estimate):
    whole = lambda i: (0, 0)
    lead, _, wide = came.shape
    own = lambda i: (4 + i, 0)
    return pl.pallas_call(
        fold_kernel,
        grid=(4,),
        in_specs=[
            pl.BlockSpec(forth.shape, whole, pipeline_mode=ONCE),
            pl.BlockSpec(back.shape, whole, pipeline_mode=ONCE),
            pl.BlockSpec((256, TOKENS), own),
            pl.BlockSpec((256, TOKENS), own),
            pl.BlockSpec((lead, 256, wide), lambda i: (0, i, 0)),
        ],
        out_specs=[pl.BlockSpec((lead, n, wide), lambda i: (0, 0, 0)) for n in sizes],
        out_shape=[shape((lead, n, wide), BF16) for n in sizes],
        compiler_params=params(60),
        cost_estimate=cost(estimate),
        name="fold",
    )(forth, back, normed_t, grad_t, came)


def mlp_kernel(normed, grad, normed_t, grad_t, up, down, bias, weight_grad, branch, back, bias_grad, ups, downs, actives, grads):
    step = pl.program_id(0)

    @pl.when(step < 4)
    def _():
        hidden = dot(normed[...], up[...]) + bias[...]
        square = hidden * hidden
        slope = 0.7978845608028654
        turn = jnp.tanh(slope * (hidden + 0.044715 * (square * hidden)))
        half = 0.5 * (1.0 + turn)
        derivative = half + 0.5 * hidden * (1.0 - turn * turn) * (slope * (1.0 + 0.134145 * square))
        grad_hidden = (dot(grad[...], down[...]) * derivative).astype(BF16)
        columns = lane_block(step, 256)
        actives[:, columns] = (hidden * half).astype(BF16)
        grads[:, columns] = grad_hidden
        ups[:, columns] = up[...]
        downs[:, columns] = down[...]
        bias_grad[...] = jnp.sum(grad_hidden.astype(F32), axis=0, keepdims=True)

    @pl.when(step >= 4)
    def _():
        rows = lane_block(step - 4, 512)
        branch[...] = dot_nt(actives[...], downs[rows, :]).astype(BF16)
        back[...] = dot_nt(grads[...], ups[rows, :]).astype(BF16)
        weight_grad[0] = dot(normed_t[...], grads[...]).astype(BF16)
        weight_grad[1] = dot(grad_t[...], actives[...]).astype(BF16)


def mlp_call(normed, grad, normed_t, grad_t, weight, base, bias):
    whole = lambda i: (0, 0)
    early = lambda i: jnp.minimum(i, 3)
    late = lambda i: jnp.maximum(i - 4, 0)
    return pl.pallas_call(
        mlp_kernel,
        grid=(8,),
        in_specs=[
            pl.BlockSpec((TOKENS, WIDTH), whole, pipeline_mode=ONCE),
            pl.BlockSpec((TOKENS, WIDTH), whole, pipeline_mode=ONCE),
            pl.BlockSpec((512, TOKENS), lambda i: (late(i), 0)),
            pl.BlockSpec((512, TOKENS), lambda i: (late(i), 0)),
            pl.BlockSpec((WIDTH, 256), lambda i: (0, base + early(i))),
            pl.BlockSpec((WIDTH, 256), lambda i: (0, base + 4 + early(i))),
            pl.BlockSpec((1, 256), lambda i: (0, early(i))),
        ],
        out_specs=[
            pl.BlockSpec((2, 512, 1024), lambda i: (0, late(i), 0)),
            pl.BlockSpec((TOKENS, 512), lambda i: (0, late(i))),
            pl.BlockSpec((TOKENS, 512), lambda i: (0, late(i))),
            pl.BlockSpec((1, 256), lambda i: (0, early(i))),
        ],
        out_shape=[
            shape((2, WIDTH, 1024), BF16),
            shape((TOKENS, WIDTH), BF16),
            shape((TOKENS, WIDTH), BF16),
            shape((1, 1024), F32),
        ],
        scratch_shapes=[
            pltpu.VMEM((WIDTH, 1024), BF16),
            pltpu.VMEM((WIDTH, 1024), BF16),
            pltpu.VMEM((TOKENS, 1024), BF16),
            pltpu.VMEM((TOKENS, 1024), BF16),
        ],
        compiler_params=params(60),
        cost_estimate=cost(12),
        name="mlp",
    )(normed, grad, normed_t, grad_t, weight, weight, bias)


def collect_kernel(where, q0, q1, q2, q3, normed_t, grad_t, grads, contexts, bias_grad, other):
    for k, ref in enumerate((q0, q1, q2, q3)):
        group = lax.rem(where[1] + k, 4)
        grads[:, lane_block(group, 384)] = ref[:, :384]
        contexts[:, lane_block(group, 128)] = ref[:, 384:]
    bias_grad[...] = jnp.sum(grads[...].astype(F32), axis=0, keepdims=True)
    other[0, :, :1536] = dot(normed_t[...], grads[...]).astype(BF16)
    other[0, :, 1536:] = dot(grad_t[...], contexts[...]).astype(BF16)


def collect_call(where, pieces, normed_t, grad_t):
    return pl.pallas_call(
        collect_kernel,
        grid=(1,),
        in_specs=[SMEM_SPEC] + [pl.BlockSpec((TOKENS, 512), lambda i: (0, 0))] * 4
        + [pl.BlockSpec((1024, TOKENS), lambda i: (0, 0))] * 2,
        out_specs=[VMEM_SPEC] * 4,
        out_shape=[
            shape((TOKENS, 1536), BF16),
            shape((TOKENS, 512), BF16),
            shape((1, 1536), F32),
            shape((1, 1024, WIDTH), BF16),
        ],
        compiler_params=params(60),
        cost_estimate=cost(4),
        name="collect",
    )(where, *pieces, normed_t, grad_t)


def close_kernel(
    where, context, grad_qkv, w_dense, w_qkv, b0, b1, g0, g1, rows, stats, gain,
    w0, w1, w2, w3, tails, raws, standards, branches, sums,
):
    step = pl.program_id(0)
    lane = lax.broadcasted_iota(jnp.int32, (TOKENS, 128), 1)

    @pl.when(step == 0)
    def _():
        sums[...] = jnp.zeros((TOKENS, 128), F32)

    @pl.when(step < 4)
    def _():
        branch = dot_nt(context[...], w_dense[...]) + b0[...].astype(F32) + b1[...].astype(F32)
        branches[step] = branch.astype(BF16)
        raw = dot_nt(grad_qkv[...], w_qkv[...]) + g0[...].astype(F32) + g1[...].astype(F32)
        scaled = raw * gain[step]
        raws[step] = scaled
        standard = (rows[...].astype(F32) - stats[:, 0:1]) * stats[:, 1:2]
        standards[step] = standard
        first = jnp.sum(scaled, axis=1, keepdims=True)
        second = jnp.sum(scaled * standard, axis=1, keepdims=True)
        sums[...] += jnp.where(lane == 0, first, second) * (1.0 / WIDTH)
        row = lax.broadcasted_iota(jnp.int32, (8, 512), 0)
        gain_sum = jnp.sum(raw * standard, axis=0, keepdims=True)
        tails[...] = jnp.where(row == 0, gain_sum, jnp.sum(raw, axis=0, keepdims=True))

    for k, out in enumerate((w0, w1, w2, w3)):

        @pl.when(step == 4 + k)
        def _(out=out, k=k):
            block = lax.rem(where[0] + k, 4)
            whole = raws[block] - sums[:, 0:1] - standards[block] * sums[:, 1:2]
            out[0:512, :] = (stats[:, 1:2] * whole).astype(BF16)
            out[512:1024, :] = branches[block]


def close_call(where, context, grad_qkv, weight, branches, backs, rows, stats, gain):
    whole = lambda i: (0, 0)
    row = lambda i: jnp.minimum(i, 3)
    column = pl.BlockSpec((TOKENS, 512), lambda i: (0, row(i)))
    sizes = (1024,) * 4
    return pl.pallas_call(
        close_kernel,
        grid=(8,),
        in_specs=[
            SMEM_SPEC,
            pl.BlockSpec((TOKENS, 512), whole, pipeline_mode=ONCE),
            pl.BlockSpec((TOKENS, 1536), whole, pipeline_mode=ONCE),
            pl.BlockSpec((512, 512), lambda i: (row(i), 3)),
            pl.BlockSpec((512, 1536), lambda i: (row(i), 0)),
        ]
        + [column] * 5
        + [
            pl.BlockSpec((TOKENS, 128), whole, pipeline_mode=ONCE),
            pl.BlockSpec((4, 1, 512), lambda i: (0, 0, 0), pipeline_mode=ONCE),
        ],
        out_specs=[pl.BlockSpec((n, 512), whole) for n in sizes] + [pl.BlockSpec((8, 512), lambda i: (0, row(i)))],
        out_shape=[shape((n, 512), BF16) for n in sizes] + [shape((8, WIDTH), F32)],
        scratch_shapes=[
            pltpu.VMEM((4, TOKENS, 512), F32),
            pltpu.VMEM((4, TOKENS, 512), F32),
            pltpu.VMEM((4, TOKENS, 512), BF16),
            pltpu.VMEM((TOKENS, 128), F32),
        ],
        compiler_params=params(60),
        cost_estimate=cost(15),
        name="close",
    )(where, context, grad_qkv, weight, weight, *branches, *backs, rows, stats, gain)


def rotary_tables(segments):
    position = jnp.arange(LENGTH, dtype=jnp.int32)[None, :]
    one = jnp.sum((segments < 1).astype(jnp.int32), axis=1, keepdims=True)
    two = jnp.sum((segments < 2).astype(jnp.int32), axis=1, keepdims=True)
    low = jnp.where(segments == 0, 0, jnp.where(segments == 1, one, two))
    exponent = jnp.arange(ROT // 2, dtype=F32) * (2.0 / ROT)
    frequency = jnp.power(10000.0, -exponent)
    angles = (position - low).astype(F32)[:, None, :] * frequency[None, :, None]
    return jnp.broadcast_to(low[:, None, :], (low.shape[0], 8, LENGTH)), jnp.cos(angles), jnp.sin(angles)


def add(*arrays):
    total = arrays[0].astype(F32)
    for array in arrays[1:]:
        total = total + array.astype(F32)
    return total


def shift_y(array, step):
    return lax.ppermute(array, "fsdp", [(i, (i + 2 * step) % 8) for i in range(8)])


def swap_core(array):
    return lax.ppermute(array, "fsdp", [(i, i ^ 1) for i in range(8)])


def after(value, *others):
    return lax.optimization_barrier((value,) + others)[0]


def sum_x(parts):
    return [add(*(p[:, 64 * k : 64 * k + 64] for p in parts)).astype(BF16) for k in range(4)]


def local(tokens, segments, gain, shift_, w_qkv, b_qkv, w_dense, b_dense, w_fc1, b_fc1, w_fc2, b_fc2, cotangent):
    x = lax.axis_index("ctx").astype(jnp.int32)
    z = lax.axis_index("tp").astype(jnp.int32)
    f = lax.axis_index("fsdp").astype(jnp.int32)
    seqs = tokens.shape[0]
    mine = tokens.reshape(TOKENS, 512)
    grad = cotangent.reshape(TOKENS, 512)
    where = jnp.stack([z, x, f // 2, f % 2])

    early = pick_call(where[1:2], w_qkv, w_dense, w_fc1, w_fc2)
    early, mine, grad, gain = lax.optimization_barrier((early, mine, grad, gain))
    wa = lax.all_gather(early, ("fsdp", "ctx"), axis=0, tiled=True)
    affine = jnp.stack(split_three(gain) + split_three(shift_) + [jnp.zeros((512,), BF16)] * 10)
    send = jnp.concatenate([mine, affine], axis=0)

    t1, t3 = shift(send, "tp", 1), shift(send, "tp", 3)
    g1, g3 = shift(grad, "tp", 1), shift(grad, "tp", 3)
    t2 = shift(t1, "tp", 1)
    g2 = shift(g3, "tp", 3)
    normed, normed_n, normed_s, rows, stats, gain_full = norm_call(where, [send, t1, t2, t3])
    grad_full, grad_n, grad_s = join_call(where, [grad, g1, g2, g3])

    late = jnp.concatenate([w_fc1[:, 1024:], w_fc2[:, 1024:]], axis=1)
    order = (x + jnp.arange(4, dtype=jnp.int32)) % 4
    bias = b_qkv.reshape(1, 1536)
    bias_ff = [b_fc1[:1024].reshape(1, 1024), b_fc1[1024:].reshape(1, 1024)]
    tables = rotary_tables(segments)
    normed, grad_full, late, tables, order, bias, bias_ff = lax.optimization_barrier(
        (normed, grad_full, late, tables, order, bias, bias_ff)
    )
    low, cosine, sine = tables
    late, wa, normed = lax.optimization_barrier((late, wa, normed))
    wb = lax.all_gather(late, "fsdp", axis=0, tiled=True)

    kept, *sent = project_call(order, normed, grad_full, wa, bias, 12)
    arrived = [shift(a, "ctx", k + 1) for k, a in enumerate(sent)]
    ff0 = mlp_call(after(normed, kept), grad_full, normed_n, grad_n, wa, 8, bias_ff[0])
    *arrived, f0 = lax.optimization_barrier((kept, *arrived, ff0[0]))
    f0 = lax.psum_scatter(f0, "fsdp", scatter_dimension=1, tiled=True)
    done = attention_call(where[1:2], [a.reshape(seqs, ROWS, 512) for a in arrived], low, cosine, sine)
    done = [a.reshape(TOKENS, 512) for a in done]
    returned = [done[0]] + [shift(a, "ctx", 4 - k) for k, a in enumerate(done) if k > 0]
    ff1 = mlp_call(after(normed, done[0]), grad_full, normed_n, grad_n, wb, 0, bias_ff[1])
    *returned, f1 = lax.optimization_barrier((*returned, ff1[0]))
    f1 = lax.psum_scatter(f1, "fsdp", scatter_dimension=1, tiled=True)
    grad_qkv, context, bias_grad_a, other_a = collect_call(where, returned, normed_s, grad_s)
    came_a = swap_core(other_a)
    *w, tails = close_call(
        where[0:1],
        after(context, other_a),
        grad_qkv,
        wa,
        [ff0[1], ff1[1]],
        [ff0[2], ff1[2]],
        rows,
        stats,
        gain_full,
    )
    w1, w3 = shift(w[1], "tp", 1), shift(w[3], "tp", 3)
    a = fold_call(after(context, w[0]), grad_qkv, normed_s, grad_s, came_a, (256,) * 4, 30)
    xa1, xa3 = shift(a[1], "ctx", 1), shift(a[3], "ctx", 3)
    small = jnp.concatenate(
        [tails[0:2].reshape(4096), jnp.sum(grad.astype(F32), axis=0), bias_grad_a[0], ff0[3][0], ff1[3][0]]
    )
    small = after(small, a[0])
    small = small + swap_core(small)
    xa1, xa3, w1, w3, small, a2, w2 = lax.optimization_barrier((xa1, xa3, w1, w3, small, a[2], w[2]))
    xa2, w2 = shift(a2, "ctx", 2), shift(w2, "tp", 2)
    small = small + shift_y(small, 1) + shift_y(small, 2) + shift_y(small, 3)
    xa2, w2, small, f0, f1 = lax.optimization_barrier((xa2, w2, small, f0, f1))
    f01 = lax.psum_scatter(jnp.concatenate([f0, f1]), "ctx", scatter_dimension=1, tiled=True)
    total = add(w[0], w1, w2, w3)
    ja = sum_x([a[0], xa1, xa2, xa3])
    y1, y3 = shift_y(ja[1], 1), shift_y(ja[3], 3)
    small = small + shift(small, "ctx", 1) + shift(small, "ctx", 2) + shift(small, "ctx", 3)
    y1, y3, small, j2 = lax.optimization_barrier((y1, y3, small, ja[2]))
    y2 = shift_y(j2, 2)
    both = small[:4096]
    both = both + shift(both, "tp", 1) + shift(both, "tp", 2) + shift(both, "tp", 3)
    y2, both, f01 = lax.optimization_barrier((y2, both, f01))
    grad_tokens = (grad.astype(F32) + total[:512]).reshape(tokens.shape)
    mixed = (mine.astype(F32) + total[512:] + b_dense + b_fc2).astype(BF16).reshape(tokens.shape)

    f01 = f01.astype(F32)
    ga = add(ja[0], y1, y2, y3)[0]
    grad_w_fc1 = jnp.concatenate([f01[0], f01[2]], axis=1)
    grad_w_fc2 = jnp.concatenate([f01[1], f01[3]], axis=1)
    both = lax.dynamic_index_in_dim(both.reshape(2, 4, 512), z, 1, keepdims=False)
    small = small[4096:]
    grad_b_out = small[:512]
    return (
        mixed,
        grad_tokens,
        both[0],
        both[1],
        ga[:, :1536],
        small[512:2048],
        ga[:, 1536:],
        grad_b_out,
        grad_w_fc1,
        small[2048:],
        grad_w_fc2,
        grad_b_out,
    )


def solution(mesh):
    token = P("fsdp", "ctx", "tp")
    weight = P("fsdp", "tp")
    weight_grad = P(("fsdp", "ctx"), "tp")
    vector = P("tp")
    return jax.shard_map(
        local,
        mesh=mesh,
        in_specs=(
            token, P("fsdp", None), vector, vector, weight, vector, weight, vector, weight, vector, weight, vector, token,
        ),
        out_specs=(
            token, token, vector, vector, weight_grad, vector, weight_grad, vector, weight_grad, vector, weight_grad, vector,
        ),
        check_vma=False,
    )
```

```python
import jax
import jax.numpy as jnp
from jax import lax
from jax.experimental import pallas as pl
from jax.experimental.pallas import tpu as pltpu
from jax.sharding import PartitionSpec as P

WIDTH = 2048
ROT = 32
HEAD = 64
LENGTH = 1024
ROWS = 256
TOKENS = 512
EPSILON = 1e-05
MASKED = -1000000000.0
F32 = jnp.float32
BF16 = jnp.bfloat16
MEBI = 1024 * 1024


def dot(a, b):
    return lax.dot_general(a, b, (((1,), (0,)), ((), ())), preferred_element_type=F32)


def dot_nt(a, b):
    return lax.dot_general(a, b, (((1,), (1,)), ((), ())), preferred_element_type=F32)


def shift(array, axis, step):
    return lax.ppermute(array, axis, [(i, (i + step) % 4) for i in range(4)])


def params(mebi):
    return pltpu.CompilerParams(vmem_limit_bytes=mebi * MEBI)


def cost(microseconds):
    return pl.CostEstimate(flops=int(microseconds * 1.15e9), bytes_accessed=1024, transcendentals=0)


def lane_block(index, width):
    return pl.ds(pl.multiple_of(index * width, 128), width)


def place_rows(where, block, piece, natural, sorted_):
    turned = piece.T
    natural[lane_block(block, 512), :] = turned
    for core in range(2):
        for column in range(4):
            to_core = 1 - (where[3] ^ core)
            to_x = lax.rem(column + 4 - where[1], 4)
            to_y = lax.rem(block + 4 - where[2], 4)
            row = ((to_core * 4 + to_x) * 4 + to_y) * 64
            first = (core * 4 + column) * 64
            sorted_[pl.ds(pl.multiple_of(row, 64), 64), :] = turned[first : first + 64]


def norm_kernel(where, t0, t1, t2, t3, normed, natural, sorted_, rows, stats, gains):
    tokens = (t0, t1, t2, t3)
    total = jnp.zeros((TOKENS, 1), F32)
    for ref in tokens:
        total += jnp.sum(ref[:TOKENS, :].astype(F32), axis=1, keepdims=True)
    mean = total * (1.0 / WIDTH)
    square = jnp.zeros((TOKENS, 1), F32)
    for ref in tokens:
        centred = ref[:TOKENS, :].astype(F32) - mean
        square += jnp.sum(centred * centred, axis=1, keepdims=True)
    inverse = lax.rsqrt(square * (1.0 / WIDTH) + EPSILON)
    lane = lax.broadcasted_iota(jnp.int32, (TOKENS, 128), 1)
    stats[...] = jnp.where(lane == 0, mean, inverse)
    for k, ref in enumerate(tokens):
        block = lax.rem(where[0] + 4 - k, 4)
        affine = ref[TOKENS:, :].astype(F32)
        gain = (affine[0:1] + affine[1:2]) + affine[2:3]
        bias = (affine[3:4] + affine[4:5]) + affine[5:6]
        gains[block] = gain
        piece = ref[:TOKENS, :]
        rows[:, lane_block(block, 512)] = piece
        scaled = (piece.astype(F32) - mean) * inverse
        out = (scaled * gain + bias).astype(BF16)
        normed[:, lane_block(block, 512)] = out
        place_rows(where, block, out, natural, sorted_)


def join_kernel(where, t0, t1, t2, t3, full, natural, sorted_):
    for k, ref in enumerate((t0, t1, t2, t3)):
        block = lax.rem(where[0] + 4 - k, 4)
        piece = ref[...]
        full[:, lane_block(block, 512)] = piece
        place_rows(where, block, piece, natural, sorted_)


ONCE = pl.Buffered(1)
SMEM_SPEC = pl.BlockSpec(memory_space=pltpu.SMEM)
VMEM_SPEC = pl.BlockSpec(memory_space=pltpu.VMEM)


def shape(dims, dtype):
    return jax.ShapeDtypeStruct(dims, dtype)


def split_three(value):
    parts = []
    for _ in range(3):
        part = lax.reduce_precision(value, exponent_bits=8, mantissa_bits=7)
        parts.append(part.astype(BF16))
        value = value - part
    return parts


def norm_call(where, tokens):
    return pl.pallas_call(
        norm_kernel,
        out_shape=(
            shape((TOKENS, WIDTH), BF16),
            shape((WIDTH, TOKENS), BF16),
            shape((WIDTH, TOKENS), BF16),
            shape((TOKENS, WIDTH), BF16),
            shape((TOKENS, 128), F32),
            shape((4, 1, 512), F32),
        ),
        in_specs=[SMEM_SPEC] + [VMEM_SPEC] * 4,
        out_specs=[VMEM_SPEC] * 6,
        compiler_params=params(63),
        cost_estimate=cost(7),
        name="norm",
    )(where, *tokens)


def join_call(where, pieces):
    return pl.pallas_call(
        join_kernel,
        out_shape=(shape((TOKENS, WIDTH), BF16), shape((WIDTH, TOKENS), BF16), shape((WIDTH, TOKENS), BF16)),
        in_specs=[SMEM_SPEC] + [VMEM_SPEC] * 4,
        out_specs=[VMEM_SPEC] * 3,
        compiler_params=params(63),
        cost_estimate=cost(5),
        name="join",
    )(where, *pieces)


def pick_kernel(where, w_qkv, w_dense, w_fc1, w_fc2, out):
    out[:, 0:1536] = w_qkv[...]
    out[:, 1536:2048] = w_dense[...]
    out[:, 2048:3072] = w_fc1[...]
    out[:, 3072:4096] = w_fc2[...]


def pick_call(x, w_qkv, w_dense, w_fc1, w_fc2):
    here = lambda i, x: (x[0], 0)
    return pl.pallas_call(
        pick_kernel,
        grid_spec=pltpu.PrefetchScalarGridSpec(
            num_scalar_prefetch=1,
            grid=(1,),
            in_specs=[pl.BlockSpec((64, n), here) for n in (1536, 512, 1024, 1024)],
            out_specs=pl.BlockSpec((64, 4096), lambda i, x: (0, 0)),
        ),
        out_shape=shape((64, 4096), BF16),
        compiler_params=params(63),
        cost_estimate=cost(1),
        name="pick",
    )(x, w_qkv, w_dense, w_fc1, w_fc2)


def project_kernel(where, normed, grad, w_qkv, w_dense, bias, *outs):
    step = pl.program_id(0)
    qkv = (dot(normed[...], w_qkv[...]) + bias[...]).astype(BF16)
    context = dot(grad[...], w_dense[...]).astype(BF16)
    for half in range(2):
        both = jnp.concatenate(
            [qkv[:, half * 384 : half * 384 + 384], context[:, half * 128 : half * 128 + 128]], axis=1
        )
        distance = lax.rem(2 * step + half + 4 - where[1], 4)
        for k, ref in enumerate(outs):

            @pl.when(distance == k)
            def _(ref=ref, both=both):
                ref[...] = both


def project_call(where, normed, grad, weight, bias):
    whole = lambda i: (0, 0)
    return pl.pallas_call(
        project_kernel,
        grid=(2,),
        in_specs=[
            SMEM_SPEC,
            pl.BlockSpec((TOKENS, WIDTH), whole, pipeline_mode=ONCE),
            pl.BlockSpec((TOKENS, WIDTH), whole, pipeline_mode=ONCE),
            pl.BlockSpec((WIDTH, 768), lambda i: (0, i)),
            pl.BlockSpec((WIDTH, 256), lambda i: (0, 6 + i)),
            pl.BlockSpec((1, 768), lambda i: (0, i)),
        ],
        out_specs=[pl.BlockSpec((TOKENS, 512), whole)] * 4,
        out_shape=[shape((TOKENS, 512), BF16)] * 4,
        compiler_params=params(63),
        cost_estimate=cost(12),
        name="project",
    )(where, normed, grad, weight, weight, bias)


def half_swap(u, lane):
    return jnp.where((lane & 31) < 16, pltpu.roll(u, 112, 1), pltpu.roll(u, 16, 1))


def attention_kernel(where, a0, a1, a2, a3, low, narrow_c, narrow_s, o0, o1, o2, o3, slab, slab_t, masked, turned, grad_k, grad_v, cosine, sine):
    lane = lax.broadcasted_iota(jnp.int32, (ROWS, 128), 1)
    left = lane < HEAD
    for i in range(4):
        place = slice(i * ROWS, (i + 1) * ROWS)
        c = narrow_c[0, :, place]
        s = narrow_s[0, :, place]
        one = jnp.ones((32, ROWS), F32)
        cosine[place, :] = jnp.concatenate([c, c, one, c, c, one], axis=0).T
        one = jnp.zeros((32, ROWS), F32)
        sine[place, :] = jnp.concatenate([-s, s, one, -s, s, one], axis=0).T
    for k, ref in enumerate((a0, a1, a2, a3)):
        block = lax.rem(where[0] + 4 - k, 4)
        place = pl.ds(pl.multiple_of(block * ROWS, ROWS), ROWS)
        c = cosine[place, :]
        s = sine[place, :]
        u = ref[0, :, 0:128].astype(F32)
        rotated = u * c + half_swap(u, lane) * s
        first = jnp.where(left, rotated * 0.125, rotated).astype(BF16)
        u = ref[0, :, 128:256].astype(F32)
        rotated = u * c + half_swap(u, lane) * s
        second = jnp.where(left, u, rotated * 0.125).astype(BF16)
        u = ref[0, :, 256:384].astype(F32)
        rotated = u * c + half_swap(u, lane) * s
        third = jnp.where(left, rotated, u).astype(BF16)
        fourth = ref[0, :, 384:512]
        slab[place, 0:128] = first
        slab[place, 128:256] = second
        slab[place, 256:384] = third
        slab[place, 384:512] = fourth
        zero = jnp.zeros((ROWS, 128), BF16)
        masked[place, 0:128] = jnp.where(left, first, zero)
        masked[place, 128:256] = jnp.where(left, zero, second)
        masked[place, 256:384] = jnp.where(left, fourth, zero)
        masked[place, 384:512] = jnp.where(left, zero, fourth)
    for i in range(4):
        place = slice(i * ROWS, (i + 1) * ROWS)
        for j in range(4):
            slab_t[j * 128 : (j + 1) * 128, place] = slab[place, j * 128 : (j + 1) * 128].T
    zeros = jnp.zeros((HEAD, ROWS), BF16)
    for i in range(4):
        own = slice(i * ROWS, (i + 1) * ROWS)
        end = (i + 1) * ROWS
        start = low[0, 0:1, own]
        key = lax.broadcasted_iota(jnp.int32, (ROWS, ROWS), 0)
        query = lax.broadcasted_iota(jnp.int32, (ROWS, ROWS), 1)
        causal = key <= query
        for h in range(2):
            if h == 0:
                keys = slab[0:end, 0:128]
                values = slab[0:end, 128:256]
                query_t = jnp.concatenate([zeros, slab_t[0:64, own]], axis=0)
                grad_t = jnp.concatenate([slab_t[384:448, own], zeros], axis=0)
                key_rows, value_rows = slice(64, 128), slice(128, 192)
            else:
                keys = slab[0:end, 256:384]
                values = slab[0:end, 256:384]
                query_t = jnp.concatenate([slab_t[192:256, own], zeros], axis=0)
                grad_t = jnp.concatenate([zeros, slab_t[448:512, own]], axis=0)
                key_rows, value_rows = slice(256, 320), slice(320, 384)
            score = dot(keys, query_t)
            pieces = []
            for j in range(i + 1):
                piece = score[j * ROWS : (j + 1) * ROWS]
                allowed = None
                if j == 0 or i == 3:
                    allowed = key + j * ROWS >= start
                if j == i:
                    allowed = causal if allowed is None else allowed & causal
                if allowed is not None:
                    piece = jnp.where(allowed, piece, MASKED)
                pieces.append(piece)
            score = jnp.concatenate(pieces, axis=0) if len(pieces) > 1 else pieces[0]
            largest = jnp.max(score, axis=0, keepdims=True)
            weight = jnp.exp(score - largest)
            total = jnp.sum(weight, axis=0, keepdims=True)
            weight = weight * (1.0 / total)
            rounded = weight.astype(BF16)
            grad_weight = dot(values, grad_t)
            inner = jnp.sum(weight * grad_weight, axis=0, keepdims=True)
            grad_score = (weight * (grad_weight - inner)).astype(BF16)
            turned[h * 64 : h * 64 + 64, own] = dot(slab_t[key_rows, 0:end], grad_score)
            turned[128 + h * 64 : 192 + h * 64, own] = dot(slab_t[value_rows, 0:end], rounded)
            add_k = dot(grad_score, masked[own, h * 128 : (h + 1) * 128])
            add_v = dot(rounded, masked[own, 256 + h * 128 : 384 + h * 128])
            if h == 0:
                new_k, new_v = add_k, add_v
            else:
                new_k, new_v = new_k + add_k, new_v + add_v
        if i > 0:
            before = slice(0, i * ROWS)
            grad_k[before, :] += new_k[0 : i * ROWS]
            grad_v[before, :] += new_v[0 : i * ROWS]
        grad_k[own, :] = new_k[i * ROWS :]
        grad_v[own, :] = new_v[i * ROWS :]
    for k, ref in enumerate((o0, o1, o2, o3)):
        block = lax.rem(where[0] + 4 - k, 4)
        place = pl.ds(pl.multiple_of(block * ROWS, ROWS), ROWS)
        c = cosine[place, :]
        s = sine[place, :]
        gq = turned[0:128, place].T * 0.125
        gq = gq * c - half_swap(gq, lane) * s
        gk = grad_k[place, :]
        gk = gk * c - half_swap(gk, lane) * s
        gv = grad_v[place, :]
        gk = pltpu.roll(gk, 64, 1)
        ref[0, :, 0:128] = jnp.where(left, gq, gk).astype(BF16)
        ref[0, :, 128:256] = jnp.where(left, gv, gq).astype(BF16)
        ref[0, :, 256:384] = jnp.where(left, gk, gv).astype(BF16)
        ref[0, :, 384:512] = turned[128:256, place].T.astype(BF16)


def attention_call(where, pieces, low, cosine, sine):
    seqs = low.shape[0]
    row = lambda i: (i, 0, 0)
    block = pl.BlockSpec((1, ROWS, 512), row)
    return pl.pallas_call(
        attention_kernel,
        grid=(seqs,),
        in_specs=[SMEM_SPEC]
        + [block] * 4
        + [
            pl.BlockSpec((1, 8, LENGTH), row),
            pl.BlockSpec((1, 16, LENGTH), row),
            pl.BlockSpec((1, 16, LENGTH), row),
        ],
        out_specs=[block] * 4,
        out_shape=[shape((seqs, ROWS, 512), BF16)] * 4,
        scratch_shapes=[
            pltpu.VMEM((LENGTH, 512), BF16),
            pltpu.VMEM((512, LENGTH), BF16),
            pltpu.VMEM((LENGTH, 512), BF16),
            pltpu.VMEM((256, LENGTH), F32),
            pltpu.VMEM((LENGTH, 128), F32),
            pltpu.VMEM((LENGTH, 128), F32),
            pltpu.VMEM((LENGTH, 128), F32),
            pltpu.VMEM((LENGTH, 128), F32),
        ],
        compiler_params=params(63),
        cost_estimate=cost(8),
        name="attention",
    )(where, *pieces, low, cosine, sine)


def fold_kernel(forth, back, normed_t, grad_t, came, *outs):
    step = pl.program_id(0)
    first = dot(normed_t[...], back[...])
    second = dot(grad_t[...], forth[...])
    width = first.shape[1]
    if came.shape[0] == 2:
        first = (first + came[0].astype(F32)).astype(BF16)
        second = (second + came[1].astype(F32)).astype(BF16)
    else:
        first = (first + came[0, :, :width].astype(F32)).astype(BF16)
        second = (second + came[0, :, width:].astype(F32)).astype(BF16)

    def store(ref, rows):
        if ref.shape[0] == 2:
            ref[0] = first[rows]
            ref[1] = second[rows]
        else:
            ref[0, :, :width] = first[rows]
            ref[0, :, width:] = second[rows]

    for k in range(4):

        @pl.when(step == k)
        def _(k=k):
            if k == 0:
                store(outs[0], slice(0, 256))
            else:
                store(outs[2 * k - 1], slice(0, 128))
                store(outs[2 * k], slice(128, 256))


def fold_call(forth, back, normed_t, grad_t, came, sizes, estimate):
    whole = lambda i: (0, 0)
    lead, _, wide = came.shape
    own = lambda i: (4 + i, 0)
    return pl.pallas_call(
        fold_kernel,
        grid=(4,),
        in_specs=[
            pl.BlockSpec(forth.shape, whole, pipeline_mode=ONCE),
            pl.BlockSpec(back.shape, whole, pipeline_mode=ONCE),
            pl.BlockSpec((256, TOKENS), own),
            pl.BlockSpec((256, TOKENS), own),
            pl.BlockSpec((lead, 256, wide), lambda i: (0, i, 0)),
        ],
        out_specs=[pl.BlockSpec((lead, n, wide), lambda i: (0, 0, 0)) for n in sizes],
        out_shape=[shape((lead, n, wide), BF16) for n in sizes],
        compiler_params=params(63),
        cost_estimate=cost(estimate),
        name="fold",
    )(forth, back, normed_t, grad_t, came)


def mlp_kernel(normed, grad, normed_t, grad_t, up, down, bias, weight_grad, branch, back, bias_grad, ups, downs, actives, grads):
    step = pl.program_id(0)

    @pl.when(step < 4)
    def _():
        hidden = dot(normed[...], up[...]) + bias[...]
        square = hidden * hidden
        slope = 0.7978845608028654
        turn = jnp.tanh(slope * (hidden + 0.044715 * (square * hidden)))
        half = 0.5 * (1.0 + turn)
        derivative = half + 0.5 * hidden * (1.0 - turn * turn) * (slope * (1.0 + 0.134145 * square))
        grad_hidden = (dot(grad[...], down[...]) * derivative).astype(BF16)
        columns = lane_block(step, 256)
        actives[:, columns] = (hidden * half).astype(BF16)
        grads[:, columns] = grad_hidden
        ups[:, columns] = up[...]
        downs[:, columns] = down[...]
        bias_grad[...] = jnp.sum(grad_hidden.astype(F32), axis=0, keepdims=True)

    @pl.when(step >= 4)
    def _():
        rows = lane_block(step - 4, 512)
        branch[...] = dot_nt(actives[...], downs[rows, :]).astype(BF16)
        back[...] = dot_nt(grads[...], ups[rows, :]).astype(BF16)
        weight_grad[0] = dot(normed_t[...], grads[...]).astype(BF16)
        weight_grad[1] = dot(grad_t[...], actives[...]).astype(BF16)


def mlp_call(normed, grad, normed_t, grad_t, weight, base, bias):
    whole = lambda i: (0, 0)
    early = lambda i: jnp.minimum(i, 3)
    late = lambda i: jnp.maximum(i - 4, 0)
    return pl.pallas_call(
        mlp_kernel,
        grid=(8,),
        in_specs=[
            pl.BlockSpec((TOKENS, WIDTH), whole, pipeline_mode=ONCE),
            pl.BlockSpec((TOKENS, WIDTH), whole, pipeline_mode=ONCE),
            pl.BlockSpec((512, TOKENS), lambda i: (late(i), 0)),
            pl.BlockSpec((512, TOKENS), lambda i: (late(i), 0)),
            pl.BlockSpec((WIDTH, 256), lambda i: (0, base + early(i))),
            pl.BlockSpec((WIDTH, 256), lambda i: (0, base + 4 + early(i))),
            pl.BlockSpec((1, 256), lambda i: (0, early(i))),
        ],
        out_specs=[
            pl.BlockSpec((2, 512, 1024), lambda i: (0, late(i), 0)),
            pl.BlockSpec((TOKENS, 512), lambda i: (0, late(i))),
            pl.BlockSpec((TOKENS, 512), lambda i: (0, late(i))),
            pl.BlockSpec((1, 256), lambda i: (0, early(i))),
        ],
        out_shape=[
            shape((2, WIDTH, 1024), BF16),
            shape((TOKENS, WIDTH), BF16),
            shape((TOKENS, WIDTH), BF16),
            shape((1, 1024), F32),
        ],
        scratch_shapes=[
            pltpu.VMEM((WIDTH, 1024), BF16),
            pltpu.VMEM((WIDTH, 1024), BF16),
            pltpu.VMEM((TOKENS, 1024), BF16),
            pltpu.VMEM((TOKENS, 1024), BF16),
        ],
        compiler_params=params(63),
        cost_estimate=cost(12),
        name="mlp",
    )(normed, grad, normed_t, grad_t, weight, weight, bias)


def collect_kernel(where, q0, q1, q2, q3, normed_t, grad_t, grads, contexts, bias_grad, other):
    for k, ref in enumerate((q0, q1, q2, q3)):
        group = lax.rem(where[1] + k, 4)
        grads[:, lane_block(group, 384)] = ref[:, :384]
        contexts[:, lane_block(group, 128)] = ref[:, 384:]
    bias_grad[...] = jnp.sum(grads[...].astype(F32), axis=0, keepdims=True)
    other[0, :, :1536] = dot(normed_t[...], grads[...]).astype(BF16)
    other[0, :, 1536:] = dot(grad_t[...], contexts[...]).astype(BF16)


def collect_call(where, pieces, normed_t, grad_t):
    return pl.pallas_call(
        collect_kernel,
        grid=(1,),
        in_specs=[SMEM_SPEC] + [pl.BlockSpec((TOKENS, 512), lambda i: (0, 0))] * 4
        + [pl.BlockSpec((1024, TOKENS), lambda i: (0, 0))] * 2,
        out_specs=[VMEM_SPEC] * 4,
        out_shape=[
            shape((TOKENS, 1536), BF16),
            shape((TOKENS, 512), BF16),
            shape((1, 1536), F32),
            shape((1, 1024, WIDTH), BF16),
        ],
        compiler_params=params(63),
        cost_estimate=cost(4),
        name="collect",
    )(where, *pieces, normed_t, grad_t)


def mix_kernel(context, w_dense, b0, b1, out):
    total = dot_nt(context[...], w_dense[...]) + b0[...].astype(F32) + b1[...].astype(F32)
    out[...] = total.astype(BF16)


def mix_call(context, weight, branch0, branch1):
    column = pl.BlockSpec((TOKENS, 512), lambda i: (0, i))
    return pl.pallas_call(
        mix_kernel,
        grid=(4,),
        in_specs=[
            pl.BlockSpec((TOKENS, 512), lambda i: (0, 0), pipeline_mode=ONCE),
            pl.BlockSpec((512, 512), lambda i: (i, 3)),
            column,
            column,
        ],
        out_specs=column,
        out_shape=shape((TOKENS, WIDTH), BF16),
        compiler_params=params(63),
        cost_estimate=cost(6),
        name="mix",
    )(context, weight, branch0, branch1)


def close_kernel(
    where, grad_qkv, w_qkv, mix, g0, g1, rows, stats, gain, w0, w1, w2, w3, tails, raws, standards, branches, sums
):
    step = pl.program_id(0)
    lane = lax.broadcasted_iota(jnp.int32, (TOKENS, 128), 1)

    @pl.when(step == 0)
    def _():
        sums[...] = jnp.zeros((TOKENS, 128), F32)

    @pl.when(step < 4)
    def _():
        branches[step] = mix[...]
        raw = dot_nt(grad_qkv[...], w_qkv[...]) + g0[...].astype(F32) + g1[...].astype(F32)
        scaled = raw * gain[step]
        raws[step] = scaled
        standard = (rows[...].astype(F32) - stats[:, 0:1]) * stats[:, 1:2]
        standards[step] = standard
        first = jnp.sum(scaled, axis=1, keepdims=True)
        second = jnp.sum(scaled * standard, axis=1, keepdims=True)
        sums[...] += jnp.where(lane == 0, first, second) * (1.0 / WIDTH)
        row = lax.broadcasted_iota(jnp.int32, (8, 512), 0)
        gain_sum = jnp.sum(raw * standard, axis=0, keepdims=True)
        tails[...] = jnp.where(row == 0, gain_sum, jnp.sum(raw, axis=0, keepdims=True))

    for k, out in enumerate((w0, w1, w2, w3)):

        @pl.when(step == 4 + k)
        def _(out=out, k=k):
            block = lax.rem(where[0] + k, 4)
            whole = raws[block] - sums[:, 0:1] - standards[block] * sums[:, 1:2]
            out[0:512, :] = (stats[:, 1:2] * whole).astype(BF16)
            out[512:1024, :] = branches[block]


def close_call(where, grad_qkv, weight, mix, backs, rows, stats, gain):
    whole = lambda i: (0, 0)
    row = lambda i: jnp.minimum(i, 3)
    column = pl.BlockSpec((TOKENS, 512), lambda i: (0, row(i)))
    sizes = (1024,) * 4
    return pl.pallas_call(
        close_kernel,
        grid=(8,),
        in_specs=[
            SMEM_SPEC,
            pl.BlockSpec((TOKENS, 1536), whole, pipeline_mode=ONCE),
            pl.BlockSpec((512, 1536), lambda i: (row(i), 0)),
        ]
        + [column] * 4
        + [
            pl.BlockSpec((TOKENS, 128), whole, pipeline_mode=ONCE),
            pl.BlockSpec((4, 1, 512), lambda i: (0, 0, 0), pipeline_mode=ONCE),
        ],
        out_specs=[pl.BlockSpec((n, 512), whole) for n in sizes] + [pl.BlockSpec((8, 512), lambda i: (0, row(i)))],
        out_shape=[shape((n, 512), BF16) for n in sizes] + [shape((8, WIDTH), F32)],
        scratch_shapes=[
            pltpu.VMEM((4, TOKENS, 512), F32),
            pltpu.VMEM((4, TOKENS, 512), F32),
            pltpu.VMEM((4, TOKENS, 512), BF16),
            pltpu.VMEM((TOKENS, 128), F32),
        ],
        compiler_params=params(63),
        cost_estimate=cost(15),
        name="close",
    )(where, grad_qkv, weight, mix, *backs, rows, stats, gain)


def rotary_tables(segments):
    position = jnp.arange(LENGTH, dtype=jnp.int32)[None, :]
    one = jnp.sum((segments < 1).astype(jnp.int32), axis=1, keepdims=True)
    two = jnp.sum((segments < 2).astype(jnp.int32), axis=1, keepdims=True)
    low = jnp.where(segments == 0, 0, jnp.where(segments == 1, one, two))
    exponent = jnp.arange(ROT // 2, dtype=F32) * (2.0 / ROT)
    frequency = jnp.power(10000.0, -exponent)
    angles = (position - low).astype(F32)[:, None, :] * frequency[None, :, None]
    return jnp.broadcast_to(low[:, None, :], (low.shape[0], 8, LENGTH)), jnp.cos(angles), jnp.sin(angles)


def add(*arrays):
    total = arrays[0].astype(F32)
    for array in arrays[1:]:
        total = total + array.astype(F32)
    return total


def shift_y(array, step):
    return lax.ppermute(array, "fsdp", [(i, (i + 2 * step) % 8) for i in range(8)])


def swap_core(array):
    return lax.ppermute(array, "fsdp", [(i, i ^ 1) for i in range(8)])


def after(value, *others):
    return lax.optimization_barrier((value,) + others)[0]


def sum_x(parts):
    return [add(*(p[:, 64 * k : 64 * k + 64] for p in parts)).astype(BF16) for k in range(4)]


def spread(value, x, *others):
    value = value.reshape(2, 4, 64, 1024)
    parts = [lax.dynamic_index_in_dim(value, (x + k) % 4, 1, keepdims=False) for k in range(4)]
    return [parts[0]] + [shift(after(parts[k], *others), "ctx", k) for k in (1, 2, 3)]


def local(tokens, segments, gain, shift_, w_qkv, b_qkv, w_dense, b_dense, w_fc1, b_fc1, w_fc2, b_fc2, cotangent):
    x = lax.axis_index("ctx").astype(jnp.int32)
    z = lax.axis_index("tp").astype(jnp.int32)
    f = lax.axis_index("fsdp").astype(jnp.int32)
    seqs = tokens.shape[0]
    mine = tokens.reshape(TOKENS, 512)
    grad = cotangent.reshape(TOKENS, 512)
    where = jnp.stack([z, x, f // 2, f % 2])

    early = pick_call(where[1:2], w_qkv, w_dense, w_fc1, w_fc2)
    early, mine, grad, gain = lax.optimization_barrier((early, mine, grad, gain))
    wa = lax.all_gather(early, ("fsdp", "ctx"), axis=0, tiled=True)
    affine = jnp.stack(split_three(gain) + split_three(shift_) + [jnp.zeros((512,), BF16)] * 10)
    send = jnp.concatenate([mine, affine], axis=0)

    t1, t3 = shift(send, "tp", 1), shift(send, "tp", 3)
    g1, g3 = shift(grad, "tp", 1), shift(grad, "tp", 3)
    t2 = shift(t1, "tp", 1)
    g2 = shift(g3, "tp", 3)
    normed, normed_n, normed_s, rows, stats, gain_full = norm_call(where, [send, t1, t2, t3])
    grad_full, grad_n, grad_s = join_call(where, [grad, g1, g2, g3])

    late = jnp.concatenate([w_fc1[:, 1024:], w_fc2[:, 1024:]], axis=1)
    bias = b_qkv.reshape(1, 1536)
    bias_ff = [b_fc1[:1024].reshape(1, 1024), b_fc1[1024:].reshape(1, 1024)]
    tables = rotary_tables(segments)
    normed, grad_full, late, tables, bias, bias_ff = lax.optimization_barrier(
        (normed, grad_full, late, tables, bias, bias_ff)
    )
    low, cosine, sine = tables
    late, wa, normed = lax.optimization_barrier((late, wa, normed))
    wb = lax.all_gather(late, "fsdp", axis=0, tiled=True)

    kept, *sent = project_call(where, normed, grad_full, wa, bias)
    arrived = [shift(a, "ctx", k + 1) for k, a in enumerate(sent)]
    ff0 = mlp_call(after(normed, kept), grad_full, normed_n, grad_n, wa, 8, bias_ff[0])
    *arrived, f0 = lax.optimization_barrier((kept, *arrived, ff0[0]))
    f0 = lax.psum_scatter(f0, "fsdp", scatter_dimension=1, tiled=True)
    done = attention_call(where[1:2], [a.reshape(seqs, ROWS, 512) for a in arrived], low, cosine, sine)
    done = [a.reshape(TOKENS, 512) for a in done]
    returned = [done[0]] + [shift(a, "ctx", 4 - k) for k, a in enumerate(done) if k > 0]
    ff1 = mlp_call(after(normed, done[0]), grad_full, normed_n, grad_n, wb, 0, bias_ff[1])
    *returned, f1 = lax.optimization_barrier((*returned, ff1[0]))
    f1 = lax.psum_scatter(f1, "fsdp", scatter_dimension=1, tiled=True)
    grad_qkv, context, bias_grad_a, other_a = collect_call(where, returned, normed_s, grad_s)
    came_a = swap_core(other_a)
    mix = mix_call(after(context, other_a), wa, ff0[1], ff1[1])
    a0, a1t, a1b, a2t, a2b, a3t, a3b = fold_call(
        after(context, mix), grad_qkv, normed_s, grad_s, came_a, (256,) + (128,) * 6, 20
    )
    up, down = shift(a2t, "ctx", 1), shift(a2b, "ctx", 3)
    *w, tails = close_call(
        where[0:1], after(grad_qkv, a0), wa, mix, [ff0[2], ff1[2]], rows, stats, gain_full
    )
    up, down, w, tails = lax.optimization_barrier((up, down, w, tails))
    w1, w3 = shift(w[1], "tp", 1), shift(w[3], "tp", 3)
    small = jnp.concatenate(
        [tails[0:2].reshape(4096), jnp.sum(grad.astype(F32), axis=0), bias_grad_a[0], ff0[3][0], ff1[3][0]]
    )
    up = shift(jnp.concatenate([add(a1t, up).astype(BF16), a1b], axis=1), "ctx", 1)
    down = shift(jnp.concatenate([a3t, add(a3b, down).astype(BF16)], axis=1), "ctx", 3)
    small = small + swap_core(small)
    small = small + lax.ppermute(small, "fsdp", [(i, i ^ 2) for i in range(8)])
    small = small + lax.ppermute(small, "fsdp", [(i, i ^ 4) for i in range(8)])
    both, small = small[:4096], small[4096:]
    both = both + lax.ppermute(both, "tp", [(i, i ^ 1) for i in range(4)])
    f0 = lax.psum_scatter(after(f0, w[0]), "ctx", scatter_dimension=1, tiled=True)
    up, down, w1, w3, small, both, w2, f1 = lax.optimization_barrier((up, down, w1, w3, small, both, w[2], f1))
    ja = sum_x([a0, up, down])
    ya = [shift_y(ja[k], k) for k in (1, 2, 3)]
    w2 = shift(w2, "tp", 2)
    small = jnp.concatenate([both, small])
    small = small + lax.ppermute(small, "ctx", [(i, i ^ 1) for i in range(4)])
    ya, small = lax.optimization_barrier((ya, small))
    f1 = spread(f1, x, small)
    small = small + lax.ppermute(small, "ctx", [(i, i ^ 2) for i in range(4)])
    both, small = small[:4096], small[4096:]
    both = both + lax.ppermute(both, "tp", [(i, i ^ 2) for i in range(4)])
    both, f0, f1 = lax.optimization_barrier((both, f0, f1))
    total = add(w[0], w1, w2, w3)
    gf1 = add(*f1)
    gf0 = f0.astype(F32)
    grad_tokens = (grad.astype(F32) + total[:512]).reshape(tokens.shape)
    mixed = (mine.astype(F32) + total[512:] + b_dense + b_fc2).astype(BF16).reshape(tokens.shape)

    ga = add(ja[0], *ya)[0]
    grad_w_fc1 = jnp.concatenate([gf0[0], gf1[0]], axis=1)
    grad_w_fc2 = jnp.concatenate([gf0[1], gf1[1]], axis=1)
    both = lax.dynamic_index_in_dim(both.reshape(2, 4, 512), z, 1, keepdims=False)
    grad_b_out = small[:512]
    return (
        mixed,
        grad_tokens,
        both[0],
        both[1],
        ga[:, :1536],
        small[512:2048],
        ga[:, 1536:],
        grad_b_out,
        grad_w_fc1,
        small[2048:],
        grad_w_fc2,
        grad_b_out,
    )


def solution(mesh):
    token = P("fsdp", "ctx", "tp")
    weight = P("fsdp", "tp")
    weight_grad = P(("fsdp", "ctx"), "tp")
    vector = P("tp")
    return jax.shard_map(
        local,
        mesh=mesh,
        in_specs=(
            token, P("fsdp", None), vector, vector, weight, vector, weight, vector, weight, vector, weight, vector, token,
        ),
        out_specs=(
            token, token, vector, vector, weight_grad, vector, weight_grad, vector, weight_grad, vector, weight_grad, vector,
        ),
        check_vma=False,
    )
```

```python
import jax
import jax.numpy as jnp
from jax import lax
from jax.experimental import pallas as pl
from jax.experimental.pallas import tpu as pltpu
from jax.sharding import PartitionSpec as P

WIDTH = 2048
ROT = 32
HEAD = 64
LENGTH = 1024
ROWS = 256
TOKENS = 512
EPSILON = 1e-05
MASKED = -1000000000.0
F32 = jnp.float32
BF16 = jnp.bfloat16
MEBI = 1024 * 1024


def dot(a, b):
    return lax.dot_general(a, b, (((1,), (0,)), ((), ())), preferred_element_type=F32)


def dot_nt(a, b):
    return lax.dot_general(a, b, (((1,), (1,)), ((), ())), preferred_element_type=F32)


def shift(array, axis, step):
    return lax.ppermute(array, axis, [(i, (i + step) % 4) for i in range(4)])


def params(mebi):
    return pltpu.CompilerParams(vmem_limit_bytes=mebi * MEBI)


def cost(microseconds):
    return pl.CostEstimate(flops=int(microseconds * 1.15e9), bytes_accessed=1024, transcendentals=0)


def lane_block(index, width):
    return pl.ds(pl.multiple_of(index * width, 128), width)


def place_rows(where, block, piece, natural, sorted_):
    turned = piece.T
    natural[lane_block(block, 512), :] = turned
    for core in range(2):
        for column in range(4):
            to_core = 1 - (where[3] ^ core)
            to_x = lax.rem(column + 4 - where[1], 4)
            to_y = lax.rem(block + 4 - where[2], 4)
            row = ((to_core * 4 + to_x) * 4 + to_y) * 64
            first = (core * 4 + column) * 64
            sorted_[pl.ds(pl.multiple_of(row, 64), 64), :] = turned[first : first + 64]


def norm_kernel(where, t0, t1, t2, t3, normed, natural, sorted_, rows, stats, gains):
    tokens = (t0, t1, t2, t3)
    total = jnp.zeros((TOKENS, 1), F32)
    for ref in tokens:
        total += jnp.sum(ref[:TOKENS, :].astype(F32), axis=1, keepdims=True)
    mean = total * (1.0 / WIDTH)
    square = jnp.zeros((TOKENS, 1), F32)
    for ref in tokens:
        centred = ref[:TOKENS, :].astype(F32) - mean
        square += jnp.sum(centred * centred, axis=1, keepdims=True)
    inverse = lax.rsqrt(square * (1.0 / WIDTH) + EPSILON)
    lane = lax.broadcasted_iota(jnp.int32, (TOKENS, 128), 1)
    stats[...] = jnp.where(lane == 0, mean, inverse)
    for k, ref in enumerate(tokens):
        block = lax.rem(where[0] + 4 - k, 4)
        affine = ref[TOKENS:, :].astype(F32)
        gain = (affine[0:1] + affine[1:2]) + affine[2:3]
        bias = (affine[3:4] + affine[4:5]) + affine[5:6]
        gains[block] = gain
        piece = ref[:TOKENS, :]
        rows[:, lane_block(block, 512)] = piece
        scaled = (piece.astype(F32) - mean) * inverse
        out = (scaled * gain + bias).astype(BF16)
        normed[:, lane_block(block, 512)] = out
        place_rows(where, block, out, natural, sorted_)


def join_kernel(where, t0, t1, t2, t3, full, natural, sorted_):
    for k, ref in enumerate((t0, t1, t2, t3)):
        block = lax.rem(where[0] + 4 - k, 4)
        piece = ref[...]
        full[:, lane_block(block, 512)] = piece
        place_rows(where, block, piece, natural, sorted_)


ONCE = pl.Buffered(1)
SMEM_SPEC = pl.BlockSpec(memory_space=pltpu.SMEM)
VMEM_SPEC = pl.BlockSpec(memory_space=pltpu.VMEM)


def shape(dims, dtype):
    return jax.ShapeDtypeStruct(dims, dtype)


def split_three(value):
    parts = []
    for _ in range(3):
        part = lax.reduce_precision(value, exponent_bits=8, mantissa_bits=7)
        parts.append(part.astype(BF16))
        value = value - part
    return parts


def norm_call(where, tokens):
    return pl.pallas_call(
        norm_kernel,
        out_shape=(
            shape((TOKENS, WIDTH), BF16),
            shape((WIDTH, TOKENS), BF16),
            shape((WIDTH, TOKENS), BF16),
            shape((TOKENS, WIDTH), BF16),
            shape((TOKENS, 128), F32),
            shape((4, 1, 512), F32),
        ),
        in_specs=[SMEM_SPEC] + [VMEM_SPEC] * 4,
        out_specs=[VMEM_SPEC] * 6,
        compiler_params=params(63),
        cost_estimate=cost(7),
        name="norm",
    )(where, *tokens)


def join_call(where, pieces):
    return pl.pallas_call(
        join_kernel,
        out_shape=(shape((TOKENS, WIDTH), BF16), shape((WIDTH, TOKENS), BF16), shape((WIDTH, TOKENS), BF16)),
        in_specs=[SMEM_SPEC] + [VMEM_SPEC] * 4,
        out_specs=[VMEM_SPEC] * 3,
        compiler_params=params(63),
        cost_estimate=cost(5),
        name="join",
    )(where, *pieces)


def pick_kernel(where, w_qkv, w_dense, w_fc1, w_fc2, out):
    out[:, 0:1536] = w_qkv[...]
    out[:, 1536:2048] = w_dense[...]
    out[:, 2048:3072] = w_fc1[...]
    out[:, 3072:4096] = w_fc2[...]


def pick_call(x, w_qkv, w_dense, w_fc1, w_fc2):
    here = lambda i, x: (x[0], 0)
    return pl.pallas_call(
        pick_kernel,
        grid_spec=pltpu.PrefetchScalarGridSpec(
            num_scalar_prefetch=1,
            grid=(1,),
            in_specs=[pl.BlockSpec((64, n), here) for n in (1536, 512, 1024, 1024)],
            out_specs=pl.BlockSpec((64, 4096), lambda i, x: (0, 0)),
        ),
        out_shape=shape((64, 4096), BF16),
        compiler_params=params(63),
        cost_estimate=cost(1),
        name="pick",
    )(x, w_qkv, w_dense, w_fc1, w_fc2)


def project_kernel(where, normed, grad, w_qkv, w_dense, bias, *outs):
    step = pl.program_id(0)
    qkv = (dot(normed[...], w_qkv[...]) + bias[...]).astype(BF16)
    context = dot(grad[...], w_dense[...]).astype(BF16)
    for half in range(2):
        both = jnp.concatenate(
            [qkv[:, half * 384 : half * 384 + 384], context[:, half * 128 : half * 128 + 128]], axis=1
        )
        distance = lax.rem(2 * step + half + 4 - where[1], 4)
        for k, ref in enumerate(outs):

            @pl.when(distance == k)
            def _(ref=ref, both=both):
                ref[...] = both


def project_call(where, normed, grad, weight, bias):
    whole = lambda i: (0, 0)
    return pl.pallas_call(
        project_kernel,
        grid=(2,),
        in_specs=[
            SMEM_SPEC,
            pl.BlockSpec((TOKENS, WIDTH), whole, pipeline_mode=ONCE),
            pl.BlockSpec((TOKENS, WIDTH), whole, pipeline_mode=ONCE),
            pl.BlockSpec((WIDTH, 768), lambda i: (0, i)),
            pl.BlockSpec((WIDTH, 256), lambda i: (0, 6 + i)),
            pl.BlockSpec((1, 768), lambda i: (0, i)),
        ],
        out_specs=[pl.BlockSpec((TOKENS, 512), whole)] * 4,
        out_shape=[shape((TOKENS, 512), BF16)] * 4,
        compiler_params=params(63),
        cost_estimate=cost(12),
        name="project",
    )(where, normed, grad, weight, weight, bias)


def half_swap(u, lane):
    return jnp.where((lane & 31) < 16, pltpu.roll(u, 112, 1), pltpu.roll(u, 16, 1))


def attention_kernel(where, a0, a1, a2, a3, low, narrow_c, narrow_s, o0, o1, o2, o3, slab, slab_t, masked, turned, grad_k, grad_v, cosine, sine):
    lane = lax.broadcasted_iota(jnp.int32, (ROWS, 128), 1)
    left = lane < HEAD
    for i in range(4):
        place = slice(i * ROWS, (i + 1) * ROWS)
        c = narrow_c[0, :, place]
        s = narrow_s[0, :, place]
        one = jnp.ones((32, ROWS), F32)
        cosine[place, :] = jnp.concatenate([c, c, one, c, c, one], axis=0).T
        one = jnp.zeros((32, ROWS), F32)
        sine[place, :] = jnp.concatenate([-s, s, one, -s, s, one], axis=0).T
    for k, ref in enumerate((a0, a1, a2, a3)):
        block = lax.rem(where[0] + 4 - k, 4)
        place = pl.ds(pl.multiple_of(block * ROWS, ROWS), ROWS)
        c = cosine[place, :]
        s = sine[place, :]
        u = ref[0, :, 0:128].astype(F32)
        rotated = u * c + half_swap(u, lane) * s
        first = jnp.where(left, rotated * 0.125, rotated).astype(BF16)
        u = ref[0, :, 128:256].astype(F32)
        rotated = u * c + half_swap(u, lane) * s
        second = jnp.where(left, u, rotated * 0.125).astype(BF16)
        u = ref[0, :, 256:384].astype(F32)
        rotated = u * c + half_swap(u, lane) * s
        third = jnp.where(left, rotated, u).astype(BF16)
        fourth = ref[0, :, 384:512]
        slab[place, 0:128] = first
        slab[place, 128:256] = second
        slab[place, 256:384] = third
        slab[place, 384:512] = fourth
        zero = jnp.zeros((ROWS, 128), BF16)
        masked[place, 0:128] = jnp.where(left, first, zero)
        masked[place, 128:256] = jnp.where(left, zero, second)
        masked[place, 256:384] = jnp.where(left, fourth, zero)
        masked[place, 384:512] = jnp.where(left, zero, fourth)
    for i in range(4):
        place = slice(i * ROWS, (i + 1) * ROWS)
        for j in range(4):
            slab_t[j * 128 : (j + 1) * 128, place] = slab[place, j * 128 : (j + 1) * 128].T
    zeros = jnp.zeros((HEAD, ROWS), BF16)
    for i in range(4):
        own = slice(i * ROWS, (i + 1) * ROWS)
        end = (i + 1) * ROWS
        start = low[0, 0:1, own]
        key = lax.broadcasted_iota(jnp.int32, (ROWS, ROWS), 0)
        query = lax.broadcasted_iota(jnp.int32, (ROWS, ROWS), 1)
        causal = key <= query
        for h in range(2):
            if h == 0:
                keys = slab[0:end, 0:128]
                values = slab[0:end, 128:256]
                query_t = jnp.concatenate([zeros, slab_t[0:64, own]], axis=0)
                grad_t = jnp.concatenate([slab_t[384:448, own], zeros], axis=0)
                key_rows, value_rows = slice(64, 128), slice(128, 192)
            else:
                keys = slab[0:end, 256:384]
                values = slab[0:end, 256:384]
                query_t = jnp.concatenate([slab_t[192:256, own], zeros], axis=0)
                grad_t = jnp.concatenate([zeros, slab_t[448:512, own]], axis=0)
                key_rows, value_rows = slice(256, 320), slice(320, 384)
            score = dot(keys, query_t)
            pieces = []
            for j in range(i + 1):
                piece = score[j * ROWS : (j + 1) * ROWS]
                allowed = None
                if j == 0 or i == 3:
                    allowed = key + j * ROWS >= start
                if j == i:
                    allowed = causal if allowed is None else allowed & causal
                if allowed is not None:
                    piece = jnp.where(allowed, piece, MASKED)
                pieces.append(piece)
            score = jnp.concatenate(pieces, axis=0) if len(pieces) > 1 else pieces[0]
            largest = jnp.max(score, axis=0, keepdims=True)
            weight = jnp.exp(score - largest)
            total = jnp.sum(weight, axis=0, keepdims=True)
            weight = weight * (1.0 / total)
            rounded = weight.astype(BF16)
            grad_weight = dot(values, grad_t)
            inner = jnp.sum(weight * grad_weight, axis=0, keepdims=True)
            grad_score = (weight * (grad_weight - inner)).astype(BF16)
            turned[h * 64 : h * 64 + 64, own] = dot(slab_t[key_rows, 0:end], grad_score)
            turned[128 + h * 64 : 192 + h * 64, own] = dot(slab_t[value_rows, 0:end], rounded)
            add_k = dot(grad_score, masked[own, h * 128 : (h + 1) * 128])
            add_v = dot(rounded, masked[own, 256 + h * 128 : 384 + h * 128])
            if h == 0:
                new_k, new_v = add_k, add_v
            else:
                new_k, new_v = new_k + add_k, new_v + add_v
        if i > 0:
            before = slice(0, i * ROWS)
            grad_k[before, :] += new_k[0 : i * ROWS]
            grad_v[before, :] += new_v[0 : i * ROWS]
        grad_k[own, :] = new_k[i * ROWS :]
        grad_v[own, :] = new_v[i * ROWS :]
    for k, ref in enumerate((o0, o1, o2, o3)):
        block = lax.rem(where[0] + 4 - k, 4)
        place = pl.ds(pl.multiple_of(block * ROWS, ROWS), ROWS)
        c = cosine[place, :]
        s = sine[place, :]
        gq = turned[0:128, place].T * 0.125
        gq = gq * c - half_swap(gq, lane) * s
        gk = grad_k[place, :]
        gk = gk * c - half_swap(gk, lane) * s
        gv = grad_v[place, :]
        gk = pltpu.roll(gk, 64, 1)
        ref[0, :, 0:128] = jnp.where(left, gq, gk).astype(BF16)
        ref[0, :, 128:256] = jnp.where(left, gv, gq).astype(BF16)
        ref[0, :, 256:384] = jnp.where(left, gk, gv).astype(BF16)
        ref[0, :, 384:512] = turned[128:256, place].T.astype(BF16)


def attention_call(where, pieces, low, cosine, sine):
    seqs = low.shape[0]
    row = lambda i: (i, 0, 0)
    block = pl.BlockSpec((1, ROWS, 512), row)
    return pl.pallas_call(
        attention_kernel,
        grid=(seqs,),
        in_specs=[SMEM_SPEC]
        + [block] * 4
        + [
            pl.BlockSpec((1, 8, LENGTH), row),
            pl.BlockSpec((1, 16, LENGTH), row),
            pl.BlockSpec((1, 16, LENGTH), row),
        ],
        out_specs=[block] * 4,
        out_shape=[shape((seqs, ROWS, 512), BF16)] * 4,
        scratch_shapes=[
            pltpu.VMEM((LENGTH, 512), BF16),
            pltpu.VMEM((512, LENGTH), BF16),
            pltpu.VMEM((LENGTH, 512), BF16),
            pltpu.VMEM((256, LENGTH), F32),
            pltpu.VMEM((LENGTH, 128), F32),
            pltpu.VMEM((LENGTH, 128), F32),
            pltpu.VMEM((LENGTH, 128), F32),
            pltpu.VMEM((LENGTH, 128), F32),
        ],
        compiler_params=params(63),
        cost_estimate=cost(8),
        name="attention",
    )(where, *pieces, low, cosine, sine)


def fold_kernel(forth, back, normed_t, grad_t, came, *outs):
    step = pl.program_id(0)
    first = dot(normed_t[...], back[...])
    second = dot(grad_t[...], forth[...])
    width = first.shape[1]
    if came.shape[0] == 2:
        first = (first + came[0].astype(F32)).astype(BF16)
        second = (second + came[1].astype(F32)).astype(BF16)
    else:
        first = (first + came[0, :, :width].astype(F32)).astype(BF16)
        second = (second + came[0, :, width:].astype(F32)).astype(BF16)

    def store(ref, rows):
        if ref.shape[0] == 2:
            ref[0] = first[rows]
            ref[1] = second[rows]
        else:
            ref[0, :, :width] = first[rows]
            ref[0, :, width:] = second[rows]

    for k in range(4):

        @pl.when(step == k)
        def _(k=k):
            if k == 0:
                store(outs[0], slice(0, 256))
            else:
                store(outs[2 * k - 1], slice(0, 128))
                store(outs[2 * k], slice(128, 256))


def fold_call(forth, back, normed_t, grad_t, came, sizes, estimate):
    whole = lambda i: (0, 0)
    lead, _, wide = came.shape
    own = lambda i: (4 + i, 0)
    return pl.pallas_call(
        fold_kernel,
        grid=(4,),
        in_specs=[
            pl.BlockSpec(forth.shape, whole, pipeline_mode=ONCE),
            pl.BlockSpec(back.shape, whole, pipeline_mode=ONCE),
            pl.BlockSpec((256, TOKENS), own),
            pl.BlockSpec((256, TOKENS), own),
            pl.BlockSpec((lead, 256, wide), lambda i: (0, i, 0)),
        ],
        out_specs=[pl.BlockSpec((lead, n, wide), lambda i: (0, 0, 0)) for n in sizes],
        out_shape=[shape((lead, n, wide), BF16) for n in sizes],
        compiler_params=params(63),
        cost_estimate=cost(estimate),
        name="fold",
    )(forth, back, normed_t, grad_t, came)


def mlp_kernel(normed, grad, normed_t, grad_t, up, down, bias, weight_grad, branch, back, bias_grad, ups, downs, actives, grads):
    step = pl.program_id(0)

    @pl.when(step < 4)
    def _():
        hidden = dot(normed[...], up[...]) + bias[...]
        square = hidden * hidden
        slope = 0.7978845608028654
        turn = jnp.tanh(slope * (hidden + 0.044715 * (square * hidden)))
        half = 0.5 * (1.0 + turn)
        derivative = half + 0.5 * hidden * (1.0 - turn * turn) * (slope * (1.0 + 0.134145 * square))
        grad_hidden = (dot(grad[...], down[...]) * derivative).astype(BF16)
        columns = lane_block(step, 256)
        actives[:, columns] = (hidden * half).astype(BF16)
        grads[:, columns] = grad_hidden
        ups[:, columns] = up[...]
        downs[:, columns] = down[...]
        bias_grad[...] = jnp.sum(grad_hidden.astype(F32), axis=0, keepdims=True)

    @pl.when(step >= 4)
    def _():
        rows = lane_block(step - 4, 512)
        branch[...] = dot_nt(actives[...], downs[rows, :]).astype(BF16)
        back[...] = dot_nt(grads[...], ups[rows, :]).astype(BF16)
        weight_grad[0] = dot(normed_t[...], grads[...]).astype(BF16)
        weight_grad[1] = dot(grad_t[...], actives[...]).astype(BF16)


def mlp_call(normed, grad, normed_t, grad_t, weight, base, bias):
    whole = lambda i: (0, 0)
    early = lambda i: jnp.minimum(i, 3)
    late = lambda i: jnp.maximum(i - 4, 0)
    return pl.pallas_call(
        mlp_kernel,
        grid=(8,),
        in_specs=[
            pl.BlockSpec((TOKENS, WIDTH), whole, pipeline_mode=ONCE),
            pl.BlockSpec((TOKENS, WIDTH), whole, pipeline_mode=ONCE),
            pl.BlockSpec((512, TOKENS), lambda i: (late(i), 0)),
            pl.BlockSpec((512, TOKENS), lambda i: (late(i), 0)),
            pl.BlockSpec((WIDTH, 256), lambda i: (0, base + early(i))),
            pl.BlockSpec((WIDTH, 256), lambda i: (0, base + 4 + early(i))),
            pl.BlockSpec((1, 256), lambda i: (0, early(i))),
        ],
        out_specs=[
            pl.BlockSpec((2, 512, 1024), lambda i: (0, late(i), 0)),
            pl.BlockSpec((TOKENS, 512), lambda i: (0, late(i))),
            pl.BlockSpec((TOKENS, 512), lambda i: (0, late(i))),
            pl.BlockSpec((1, 256), lambda i: (0, early(i))),
        ],
        out_shape=[
            shape((2, WIDTH, 1024), BF16),
            shape((TOKENS, WIDTH), BF16),
            shape((TOKENS, WIDTH), BF16),
            shape((1, 1024), F32),
        ],
        scratch_shapes=[
            pltpu.VMEM((WIDTH, 1024), BF16),
            pltpu.VMEM((WIDTH, 1024), BF16),
            pltpu.VMEM((TOKENS, 1024), BF16),
            pltpu.VMEM((TOKENS, 1024), BF16),
        ],
        compiler_params=params(63),
        cost_estimate=cost(12),
        name="mlp",
    )(normed, grad, normed_t, grad_t, weight, weight, bias)


def collect_kernel(where, q0, q1, q2, q3, normed_t, grad_t, grads, contexts, bias_grad, other):
    for k, ref in enumerate((q0, q1, q2, q3)):
        group = lax.rem(where[1] + k, 4)
        grads[:, lane_block(group, 384)] = ref[:, :384]
        contexts[:, lane_block(group, 128)] = ref[:, 384:]
    bias_grad[...] = jnp.sum(grads[...].astype(F32), axis=0, keepdims=True)
    other[0, :, :1536] = dot(normed_t[...], grads[...]).astype(BF16)
    other[0, :, 1536:] = dot(grad_t[...], contexts[...]).astype(BF16)


def collect_call(where, pieces, normed_t, grad_t):
    return pl.pallas_call(
        collect_kernel,
        grid=(1,),
        in_specs=[SMEM_SPEC] + [pl.BlockSpec((TOKENS, 512), lambda i: (0, 0))] * 4
        + [pl.BlockSpec((1024, TOKENS), lambda i: (0, 0))] * 2,
        out_specs=[VMEM_SPEC] * 4,
        out_shape=[
            shape((TOKENS, 1536), BF16),
            shape((TOKENS, 512), BF16),
            shape((1, 1536), F32),
            shape((1, 1024, WIDTH), BF16),
        ],
        compiler_params=params(63),
        cost_estimate=cost(4),
        name="collect",
    )(where, *pieces, normed_t, grad_t)


def mix_kernel(context, w_dense, b0, b1, out):
    total = dot_nt(context[...], w_dense[...]) + b0[...].astype(F32) + b1[...].astype(F32)
    out[...] = total.astype(BF16)


def mix_call(context, weight, branch0, branch1):
    column = pl.BlockSpec((TOKENS, 512), lambda i: (0, i))
    return pl.pallas_call(
        mix_kernel,
        grid=(4,),
        in_specs=[
            pl.BlockSpec((TOKENS, 512), lambda i: (0, 0), pipeline_mode=ONCE),
            pl.BlockSpec((512, 512), lambda i: (i, 3)),
            column,
            column,
        ],
        out_specs=column,
        out_shape=shape((TOKENS, WIDTH), BF16),
        compiler_params=params(63),
        cost_estimate=cost(6),
        name="mix",
    )(context, weight, branch0, branch1)


def close_kernel(
    where, grad_qkv, w_qkv, mix, g0, g1, rows, stats, gain, w0, w1, w2, w3, tails, raws, standards, branches, sums
):
    step = pl.program_id(0)
    lane = lax.broadcasted_iota(jnp.int32, (TOKENS, 128), 1)

    @pl.when(step == 0)
    def _():
        sums[...] = jnp.zeros((TOKENS, 128), F32)

    @pl.when(step < 4)
    def _():
        branches[step] = mix[...]
        raw = dot_nt(grad_qkv[...], w_qkv[...]) + g0[...].astype(F32) + g1[...].astype(F32)
        scaled = raw * gain[step]
        raws[step] = scaled
        standard = (rows[...].astype(F32) - stats[:, 0:1]) * stats[:, 1:2]
        standards[step] = standard
        first = jnp.sum(scaled, axis=1, keepdims=True)
        second = jnp.sum(scaled * standard, axis=1, keepdims=True)
        sums[...] += jnp.where(lane == 0, first, second) * (1.0 / WIDTH)
        row = lax.broadcasted_iota(jnp.int32, (8, 512), 0)
        gain_sum = jnp.sum(raw * standard, axis=0, keepdims=True)
        tails[...] = jnp.where(row == 0, gain_sum, jnp.sum(raw, axis=0, keepdims=True))

    for k, out in enumerate((w0, w1, w2, w3)):

        @pl.when(step == 4 + k)
        def _(out=out, k=k):
            block = lax.rem(where[0] + k, 4)
            whole = raws[block] - sums[:, 0:1] - standards[block] * sums[:, 1:2]
            out[0:512, :] = (stats[:, 1:2] * whole).astype(BF16)
            out[512:1024, :] = branches[block]


def close_call(where, grad_qkv, weight, mix, backs, rows, stats, gain):
    whole = lambda i: (0, 0)
    row = lambda i: jnp.minimum(i, 3)
    column = pl.BlockSpec((TOKENS, 512), lambda i: (0, row(i)))
    sizes = (1024,) * 4
    return pl.pallas_call(
        close_kernel,
        grid=(8,),
        in_specs=[
            SMEM_SPEC,
            pl.BlockSpec((TOKENS, 1536), whole, pipeline_mode=ONCE),
            pl.BlockSpec((512, 1536), lambda i: (row(i), 0)),
        ]
        + [column] * 4
        + [
            pl.BlockSpec((TOKENS, 128), whole, pipeline_mode=ONCE),
            pl.BlockSpec((4, 1, 512), lambda i: (0, 0, 0), pipeline_mode=ONCE),
        ],
        out_specs=[pl.BlockSpec((n, 512), whole) for n in sizes] + [pl.BlockSpec((8, 512), lambda i: (0, row(i)))],
        out_shape=[shape((n, 512), BF16) for n in sizes] + [shape((8, WIDTH), F32)],
        scratch_shapes=[
            pltpu.VMEM((4, TOKENS, 512), F32),
            pltpu.VMEM((4, TOKENS, 512), F32),
            pltpu.VMEM((4, TOKENS, 512), BF16),
            pltpu.VMEM((TOKENS, 128), F32),
        ],
        compiler_params=params(63),
        cost_estimate=cost(15),
        name="close",
    )(where, grad_qkv, weight, mix, *backs, rows, stats, gain)


def rotary_tables(segments):
    position = jnp.arange(LENGTH, dtype=jnp.int32)[None, :]
    one = jnp.sum((segments < 1).astype(jnp.int32), axis=1, keepdims=True)
    two = jnp.sum((segments < 2).astype(jnp.int32), axis=1, keepdims=True)
    low = jnp.where(segments == 0, 0, jnp.where(segments == 1, one, two))
    exponent = jnp.arange(ROT // 2, dtype=F32) * (2.0 / ROT)
    frequency = jnp.power(10000.0, -exponent)
    angles = (position - low).astype(F32)[:, None, :] * frequency[None, :, None]
    return jnp.broadcast_to(low[:, None, :], (low.shape[0], 8, LENGTH)), jnp.cos(angles), jnp.sin(angles)


def add(*arrays):
    total = arrays[0].astype(F32)
    for array in arrays[1:]:
        total = total + array.astype(F32)
    return total


def shift_y(array, step):
    return lax.ppermute(array, "fsdp", [(i, (i + 2 * step) % 8) for i in range(8)])


def swap_core(array):
    return lax.ppermute(array, "fsdp", [(i, i ^ 1) for i in range(8)])


def after(value, *others):
    return lax.optimization_barrier((value,) + others)[0]


def sum_x(parts):
    return [add(*(p[:, 64 * k : 64 * k + 64] for p in parts)).astype(BF16) for k in range(4)]


def spread(value, x, *others):
    value = value.reshape(2, 4, 64, 1024)
    parts = [lax.dynamic_index_in_dim(value, (x + k) % 4, 1, keepdims=False) for k in range(4)]
    return [parts[0]] + [shift(after(parts[k], *others), "ctx", k) for k in (1, 2, 3)]


def local(tokens, segments, gain, shift_, w_qkv, b_qkv, w_dense, b_dense, w_fc1, b_fc1, w_fc2, b_fc2, cotangent):
    x = lax.axis_index("ctx").astype(jnp.int32)
    z = lax.axis_index("tp").astype(jnp.int32)
    f = lax.axis_index("fsdp").astype(jnp.int32)
    seqs = tokens.shape[0]
    mine = tokens.reshape(TOKENS, 512)
    grad = cotangent.reshape(TOKENS, 512)
    where = jnp.stack([z, x, f // 2, f % 2])

    early = pick_call(where[1:2], w_qkv, w_dense, w_fc1, w_fc2)
    early, mine, grad, gain = lax.optimization_barrier((early, mine, grad, gain))
    wa = lax.all_gather(early, ("fsdp", "ctx"), axis=0, tiled=True)
    affine = jnp.stack(split_three(gain) + split_three(shift_) + [jnp.zeros((512,), BF16)] * 10)
    send = jnp.concatenate([mine, affine], axis=0)

    t1, t3 = shift(send, "tp", 1), shift(send, "tp", 3)
    g1, g3 = shift(grad, "tp", 1), shift(grad, "tp", 3)
    t2 = shift(t1, "tp", 1)
    g2 = shift(g3, "tp", 3)
    normed, normed_n, normed_s, rows, stats, gain_full = norm_call(where, [send, t1, t2, t3])
    grad_full, grad_n, grad_s = join_call(where, [grad, g1, g2, g3])

    late = jnp.concatenate([w_fc1[:, 1024:], w_fc2[:, 1024:]], axis=1)
    bias = b_qkv.reshape(1, 1536)
    bias_ff = [b_fc1[:1024].reshape(1, 1024), b_fc1[1024:].reshape(1, 1024)]
    tables = rotary_tables(segments)
    normed, grad_full, late, tables, bias, bias_ff = lax.optimization_barrier(
        (normed, grad_full, late, tables, bias, bias_ff)
    )
    low, cosine, sine = tables
    late, wa, normed = lax.optimization_barrier((late, wa, normed))
    wb = lax.all_gather(late, "fsdp", axis=0, tiled=True)

    kept, *sent = project_call(where, normed, grad_full, wa, bias)
    arrived = [shift(a, "ctx", k + 1) for k, a in enumerate(sent)]
    ff0 = mlp_call(after(normed, kept), grad_full, normed_n, grad_n, wa, 8, bias_ff[0])
    *arrived, f0 = lax.optimization_barrier((kept, *arrived, ff0[0]))
    f0 = lax.psum_scatter(f0, "fsdp", scatter_dimension=1, tiled=True)
    done = attention_call(where[1:2], [a.reshape(seqs, ROWS, 512) for a in arrived], low, cosine, sine)
    done = [a.reshape(TOKENS, 512) for a in done]
    returned = [done[0]] + [shift(a, "ctx", 4 - k) for k, a in enumerate(done) if k > 0]
    ff1 = mlp_call(after(normed, done[0]), grad_full, normed_n, grad_n, wb, 0, bias_ff[1])
    *returned, f1 = lax.optimization_barrier((*returned, ff1[0]))
    f1 = lax.psum_scatter(f1, "fsdp", scatter_dimension=1, tiled=True)
    grad_qkv, context, bias_grad_a, other_a = collect_call(where, returned, normed_s, grad_s)
    came_a = swap_core(other_a)
    mix = mix_call(after(context, other_a), wa, ff0[1], ff1[1])
    a0, a1t, a1b, a2t, a2b, a3t, a3b = fold_call(
        after(context, mix), grad_qkv, normed_s, grad_s, came_a, (256,) + (128,) * 6, 20
    )
    up, down = shift(a2t, "ctx", 1), shift(a2b, "ctx", 3)
    *w, tails = close_call(
        where[0:1], after(grad_qkv, a0), wa, mix, [ff0[2], ff1[2]], rows, stats, gain_full
    )
    up, down, w, tails = lax.optimization_barrier((up, down, w, tails))
    w1, w3 = shift(w[1], "tp", 1), shift(w[3], "tp", 3)
    small = jnp.concatenate(
        [tails[0:2].reshape(4096), jnp.sum(grad.astype(F32), axis=0), bias_grad_a[0], ff0[3][0], ff1[3][0]]
    )
    small = small + swap_core(small)
    up, down, small = lax.optimization_barrier((up, down, small))
    up = shift(jnp.concatenate([add(a1t, up).astype(BF16), a1b], axis=1), "ctx", 1)
    down = shift(jnp.concatenate([a3t, add(a3b, down).astype(BF16)], axis=1), "ctx", 3)
    small = small + lax.ppermute(small, "fsdp", [(i, i ^ 2) for i in range(8)])
    small = small + lax.ppermute(small, "fsdp", [(i, i ^ 4) for i in range(8)])
    both, small = small[:4096], small[4096:]
    both = both + lax.ppermute(both, "tp", [(i, i ^ 1) for i in range(4)])
    both = both + lax.ppermute(both, "tp", [(i, i ^ 2) for i in range(4)])
    small = jnp.concatenate([both, small])
    small = small + lax.ppermute(small, "ctx", [(i, i ^ 1) for i in range(4)])
    f0 = lax.psum_scatter(after(f0, w[0]), "ctx", scatter_dimension=1, tiled=True)
    up, down, w1, w3, small, w2, f1 = lax.optimization_barrier((up, down, w1, w3, small, w[2], f1))
    w2 = shift(w2, "tp", 2)
    ja = sum_x([a0, up, down])
    ya = [shift_y(ja[k], k) for k in (1, 2, 3)]
    small = small + lax.ppermute(small, "ctx", [(i, i ^ 2) for i in range(4)])
    ya, small = lax.optimization_barrier((ya, small))
    f1 = spread(f1, x, small)
    f0, f1 = lax.optimization_barrier((f0, f1))
    both, small = small[:4096], small[4096:]
    total = add(w[0], w1, w2, w3)
    gf1 = add(*f1)
    gf0 = f0.astype(F32)
    grad_tokens = (grad.astype(F32) + total[:512]).reshape(tokens.shape)
    mixed = (mine.astype(F32) + total[512:] + b_dense + b_fc2).astype(BF16).reshape(tokens.shape)

    ga = add(ja[0], *ya)[0]
    grad_w_fc1 = jnp.concatenate([gf0[0], gf1[0]], axis=1)
    grad_w_fc2 = jnp.concatenate([gf0[1], gf1[1]], axis=1)
    both = lax.dynamic_index_in_dim(both.reshape(2, 4, 512), z, 1, keepdims=False)
    grad_b_out = small[:512]
    return (
        mixed,
        grad_tokens,
        both[0],
        both[1],
        ga[:, :1536],
        small[512:2048],
        ga[:, 1536:],
        grad_b_out,
        grad_w_fc1,
        small[2048:],
        grad_w_fc2,
        grad_b_out,
    )


def solution(mesh):
    token = P("fsdp", "ctx", "tp")
    weight = P("fsdp", "tp")
    weight_grad = P(("fsdp", "ctx"), "tp")
    vector = P("tp")
    return jax.shard_map(
        local,
        mesh=mesh,
        in_specs=(
            token, P("fsdp", None), vector, vector, weight, vector, weight, vector, weight, vector, weight, vector, token,
        ),
        out_specs=(
            token, token, vector, vector, weight_grad, vector, weight_grad, vector, weight_grad, vector, weight_grad, vector,
        ),
        check_vma=False,
    )
```

```python
import jax
import jax.numpy as jnp
from jax import lax
from jax.experimental import pallas as pl
from jax.experimental.pallas import tpu as pltpu
from jax.sharding import PartitionSpec as P

WIDTH = 2048
ROT = 32
HEAD = 64
LENGTH = 1024
ROWS = 256
TOKENS = 512
EPSILON = 1e-05
MASKED = -1000000000.0
F32 = jnp.float32
BF16 = jnp.bfloat16
MEBI = 1024 * 1024


def dot(a, b):
    return lax.dot_general(a, b, (((1,), (0,)), ((), ())), preferred_element_type=F32)


def dot_nt(a, b):
    return lax.dot_general(a, b, (((1,), (1,)), ((), ())), preferred_element_type=F32)


def shift(array, axis, step):
    return lax.ppermute(array, axis, [(i, (i + step) % 4) for i in range(4)])


def params(mebi):
    return pltpu.CompilerParams(vmem_limit_bytes=mebi * MEBI)


def cost(microseconds):
    return pl.CostEstimate(flops=int(microseconds * 1.15e9), bytes_accessed=1024, transcendentals=0)


def lane_block(index, width):
    return pl.ds(pl.multiple_of(index * width, 128), width)


def place_rows(where, block, piece, natural, sorted_):
    turned = piece.T
    natural[lane_block(block, 512), :] = turned
    for core in range(2):
        for column in range(4):
            to_core = 1 - (where[3] ^ core)
            to_x = lax.rem(column + 4 - where[1], 4)
            to_y = lax.rem(block + 4 - where[2], 4)
            row = ((to_core * 4 + to_x) * 4 + to_y) * 64
            first = (core * 4 + column) * 64
            sorted_[pl.ds(pl.multiple_of(row, 64), 64), :] = turned[first : first + 64]


def norm_kernel(where, t0, t1, t2, t3, normed, natural, sorted_, rows, stats, gains):
    tokens = (t0, t1, t2, t3)
    total = jnp.zeros((TOKENS, 1), F32)
    for ref in tokens:
        total += jnp.sum(ref[:TOKENS, :].astype(F32), axis=1, keepdims=True)
    mean = total * (1.0 / WIDTH)
    square = jnp.zeros((TOKENS, 1), F32)
    for ref in tokens:
        centred = ref[:TOKENS, :].astype(F32) - mean
        square += jnp.sum(centred * centred, axis=1, keepdims=True)
    inverse = lax.rsqrt(square * (1.0 / WIDTH) + EPSILON)
    lane = lax.broadcasted_iota(jnp.int32, (TOKENS, 128), 1)
    stats[...] = jnp.where(lane == 0, mean, inverse)
    for k, ref in enumerate(tokens):
        block = lax.rem(where[0] + 4 - k, 4)
        affine = ref[TOKENS:, :].astype(F32)
        gain = (affine[0:1] + affine[1:2]) + affine[2:3]
        bias = (affine[3:4] + affine[4:5]) + affine[5:6]
        gains[block] = gain
        piece = ref[:TOKENS, :]
        rows[:, lane_block(block, 512)] = piece
        scaled = (piece.astype(F32) - mean) * inverse
        out = (scaled * gain + bias).astype(BF16)
        normed[:, lane_block(block, 512)] = out
        place_rows(where, block, out, natural, sorted_)


def join_kernel(where, t0, t1, t2, t3, full, natural, sorted_):
    for k, ref in enumerate((t0, t1, t2, t3)):
        block = lax.rem(where[0] + 4 - k, 4)
        piece = ref[...]
        full[:, lane_block(block, 512)] = piece
        place_rows(where, block, piece, natural, sorted_)


ONCE = pl.Buffered(1)
SMEM_SPEC = pl.BlockSpec(memory_space=pltpu.SMEM)
VMEM_SPEC = pl.BlockSpec(memory_space=pltpu.VMEM)


def shape(dims, dtype):
    return jax.ShapeDtypeStruct(dims, dtype)


def split_three(value):
    parts = []
    for _ in range(3):
        part = lax.reduce_precision(value, exponent_bits=8, mantissa_bits=7)
        parts.append(part.astype(BF16))
        value = value - part
    return parts


def norm_call(where, tokens):
    return pl.pallas_call(
        norm_kernel,
        out_shape=(
            shape((TOKENS, WIDTH), BF16),
            shape((WIDTH, TOKENS), BF16),
            shape((WIDTH, TOKENS), BF16),
            shape((TOKENS, WIDTH), BF16),
            shape((TOKENS, 128), F32),
            shape((4, 1, 512), F32),
        ),
        in_specs=[SMEM_SPEC] + [VMEM_SPEC] * 4,
        out_specs=[VMEM_SPEC] * 6,
        compiler_params=params(63),
        cost_estimate=cost(7),
        name="norm",
    )(where, *tokens)


def join_call(where, pieces):
    return pl.pallas_call(
        join_kernel,
        out_shape=(shape((TOKENS, WIDTH), BF16), shape((WIDTH, TOKENS), BF16), shape((WIDTH, TOKENS), BF16)),
        in_specs=[SMEM_SPEC] + [VMEM_SPEC] * 4,
        out_specs=[VMEM_SPEC] * 3,
        compiler_params=params(63),
        cost_estimate=cost(5),
        name="join",
    )(where, *pieces)


def pick_kernel(where, w_qkv, w_dense, w_fc1, w_fc2, out):
    out[:, 0:1536] = w_qkv[...]
    out[:, 1536:2048] = w_dense[...]
    out[:, 2048:3072] = w_fc1[...]
    out[:, 3072:4096] = w_fc2[...]


def pick_call(x, w_qkv, w_dense, w_fc1, w_fc2):
    here = lambda i, x: (x[0], 0)
    return pl.pallas_call(
        pick_kernel,
        grid_spec=pltpu.PrefetchScalarGridSpec(
            num_scalar_prefetch=1,
            grid=(1,),
            in_specs=[pl.BlockSpec((64, n), here) for n in (1536, 512, 1024, 1024)],
            out_specs=pl.BlockSpec((64, 4096), lambda i, x: (0, 0)),
        ),
        out_shape=shape((64, 4096), BF16),
        compiler_params=params(63),
        cost_estimate=cost(1),
        name="pick",
    )(x, w_qkv, w_dense, w_fc1, w_fc2)


def project_kernel(where, normed, grad, w_qkv, w_dense, bias, *outs):
    step = pl.program_id(0)
    qkv = (dot(normed[...], w_qkv[...]) + bias[...]).astype(BF16)
    context = dot(grad[...], w_dense[...]).astype(BF16)
    for half in range(2):
        both = jnp.concatenate(
            [qkv[:, half * 384 : half * 384 + 384], context[:, half * 128 : half * 128 + 128]], axis=1
        )
        distance = lax.rem(2 * step + half + 4 - where[1], 4)
        for k, ref in enumerate(outs):

            @pl.when(distance == k)
            def _(ref=ref, both=both):
                ref[...] = both


def project_call(where, normed, grad, weight, bias):
    whole = lambda i: (0, 0)
    return pl.pallas_call(
        project_kernel,
        grid=(2,),
        in_specs=[
            SMEM_SPEC,
            pl.BlockSpec((TOKENS, WIDTH), whole, pipeline_mode=ONCE),
            pl.BlockSpec((TOKENS, WIDTH), whole, pipeline_mode=ONCE),
            pl.BlockSpec((WIDTH, 768), lambda i: (0, i)),
            pl.BlockSpec((WIDTH, 256), lambda i: (0, 6 + i)),
            pl.BlockSpec((1, 768), lambda i: (0, i)),
        ],
        out_specs=[pl.BlockSpec((TOKENS, 512), whole)] * 4,
        out_shape=[shape((TOKENS, 512), BF16)] * 4,
        compiler_params=params(63),
        cost_estimate=cost(12),
        name="project",
    )(where, normed, grad, weight, weight, bias)


def half_swap(u, lane):
    return jnp.where((lane & 31) < 16, pltpu.roll(u, 112, 1), pltpu.roll(u, 16, 1))


def attention_kernel(where, a0, a1, a2, a3, low, narrow_c, narrow_s, o0, o1, o2, o3, slab, slab_t, masked, turned, grad_k, grad_v, cosine, sine):
    lane = lax.broadcasted_iota(jnp.int32, (ROWS, 128), 1)
    left = lane < HEAD
    for i in range(4):
        place = slice(i * ROWS, (i + 1) * ROWS)
        c = narrow_c[0, :, place]
        s = narrow_s[0, :, place]
        one = jnp.ones((32, ROWS), F32)
        cosine[place, :] = jnp.concatenate([c, c, one, c, c, one], axis=0).T
        one = jnp.zeros((32, ROWS), F32)
        sine[place, :] = jnp.concatenate([-s, s, one, -s, s, one], axis=0).T
    for k, ref in enumerate((a0, a1, a2, a3)):
        block = lax.rem(where[0] + 4 - k, 4)
        place = pl.ds(pl.multiple_of(block * ROWS, ROWS), ROWS)
        c = cosine[place, :]
        s = sine[place, :]
        u = ref[0, :, 0:128].astype(F32)
        rotated = u * c + half_swap(u, lane) * s
        first = jnp.where(left, rotated * 0.125, rotated).astype(BF16)
        u = ref[0, :, 128:256].astype(F32)
        rotated = u * c + half_swap(u, lane) * s
        second = jnp.where(left, u, rotated * 0.125).astype(BF16)
        u = ref[0, :, 256:384].astype(F32)
        rotated = u * c + half_swap(u, lane) * s
        third = jnp.where(left, rotated, u).astype(BF16)
        fourth = ref[0, :, 384:512]
        slab[place, 0:128] = first
        slab[place, 128:256] = second
        slab[place, 256:384] = third
        slab[place, 384:512] = fourth
        zero = jnp.zeros((ROWS, 128), BF16)
        masked[place, 0:128] = jnp.where(left, first, zero)
        masked[place, 128:256] = jnp.where(left, zero, second)
        masked[place, 256:384] = jnp.where(left, fourth, zero)
        masked[place, 384:512] = jnp.where(left, zero, fourth)
    for i in range(4):
        place = slice(i * ROWS, (i + 1) * ROWS)
        for j in range(4):
            slab_t[j * 128 : (j + 1) * 128, place] = slab[place, j * 128 : (j + 1) * 128].T
    zeros = jnp.zeros((HEAD, ROWS), BF16)
    for i in range(4):
        own = slice(i * ROWS, (i + 1) * ROWS)
        end = (i + 1) * ROWS
        start = low[0, 0:1, own]
        key = lax.broadcasted_iota(jnp.int32, (ROWS, ROWS), 0)
        query = lax.broadcasted_iota(jnp.int32, (ROWS, ROWS), 1)
        causal = key <= query
        for h in range(2):
            if h == 0:
                keys = slab[0:end, 0:128]
                values = slab[0:end, 128:256]
                query_t = jnp.concatenate([zeros, slab_t[0:64, own]], axis=0)
                grad_t = jnp.concatenate([slab_t[384:448, own], zeros], axis=0)
                key_rows, value_rows = slice(64, 128), slice(128, 192)
            else:
                keys = slab[0:end, 256:384]
                values = slab[0:end, 256:384]
                query_t = jnp.concatenate([slab_t[192:256, own], zeros], axis=0)
                grad_t = jnp.concatenate([zeros, slab_t[448:512, own]], axis=0)
                key_rows, value_rows = slice(256, 320), slice(320, 384)
            score = dot(keys, query_t)
            pieces = []
            for j in range(i + 1):
                piece = score[j * ROWS : (j + 1) * ROWS]
                allowed = None
                if j == 0 or i == 3:
                    allowed = key + j * ROWS >= start
                if j == i:
                    allowed = causal if allowed is None else allowed & causal
                if allowed is not None:
                    piece = jnp.where(allowed, piece, MASKED)
                pieces.append(piece)
            score = jnp.concatenate(pieces, axis=0) if len(pieces) > 1 else pieces[0]
            largest = jnp.max(score, axis=0, keepdims=True)
            weight = jnp.exp(score - largest)
            total = jnp.sum(weight, axis=0, keepdims=True)
            weight = weight * (1.0 / total)
            rounded = weight.astype(BF16)
            grad_weight = dot(values, grad_t)
            inner = jnp.sum(weight * grad_weight, axis=0, keepdims=True)
            grad_score = (weight * (grad_weight - inner)).astype(BF16)
            turned[h * 64 : h * 64 + 64, own] = dot(slab_t[key_rows, 0:end], grad_score)
            turned[128 + h * 64 : 192 + h * 64, own] = dot(slab_t[value_rows, 0:end], rounded)
            add_k = dot(grad_score, masked[own, h * 128 : (h + 1) * 128])
            add_v = dot(rounded, masked[own, 256 + h * 128 : 384 + h * 128])
            if h == 0:
                new_k, new_v = add_k, add_v
            else:
                new_k, new_v = new_k + add_k, new_v + add_v
        if i > 0:
            before = slice(0, i * ROWS)
            grad_k[before, :] += new_k[0 : i * ROWS]
            grad_v[before, :] += new_v[0 : i * ROWS]
        grad_k[own, :] = new_k[i * ROWS :]
        grad_v[own, :] = new_v[i * ROWS :]
    for k, ref in enumerate((o0, o1, o2, o3)):
        block = lax.rem(where[0] + 4 - k, 4)
        place = pl.ds(pl.multiple_of(block * ROWS, ROWS), ROWS)
        c = cosine[place, :]
        s = sine[place, :]
        gq = turned[0:128, place].T * 0.125
        gq = gq * c - half_swap(gq, lane) * s
        gk = grad_k[place, :]
        gk = gk * c - half_swap(gk, lane) * s
        gv = grad_v[place, :]
        gk = pltpu.roll(gk, 64, 1)
        ref[0, :, 0:128] = jnp.where(left, gq, gk).astype(BF16)
        ref[0, :, 128:256] = jnp.where(left, gv, gq).astype(BF16)
        ref[0, :, 256:384] = jnp.where(left, gk, gv).astype(BF16)
        ref[0, :, 384:512] = turned[128:256, place].T.astype(BF16)


def attention_call(where, pieces, low, cosine, sine):
    seqs = low.shape[0]
    row = lambda i: (i, 0, 0)
    block = pl.BlockSpec((1, ROWS, 512), row)
    return pl.pallas_call(
        attention_kernel,
        grid=(seqs,),
        in_specs=[SMEM_SPEC]
        + [block] * 4
        + [
            pl.BlockSpec((1, 8, LENGTH), row),
            pl.BlockSpec((1, 16, LENGTH), row),
            pl.BlockSpec((1, 16, LENGTH), row),
        ],
        out_specs=[block] * 4,
        out_shape=[shape((seqs, ROWS, 512), BF16)] * 4,
        scratch_shapes=[
            pltpu.VMEM((LENGTH, 512), BF16),
            pltpu.VMEM((512, LENGTH), BF16),
            pltpu.VMEM((LENGTH, 512), BF16),
            pltpu.VMEM((256, LENGTH), F32),
            pltpu.VMEM((LENGTH, 128), F32),
            pltpu.VMEM((LENGTH, 128), F32),
            pltpu.VMEM((LENGTH, 128), F32),
            pltpu.VMEM((LENGTH, 128), F32),
        ],
        compiler_params=params(63),
        cost_estimate=cost(8),
        name="attention",
    )(where, *pieces, low, cosine, sine)


def fold_kernel(forth, back, normed_t, grad_t, came, *outs):
    step = pl.program_id(0)
    first = dot(normed_t[...], back[...])
    second = dot(grad_t[...], forth[...])
    width = first.shape[1]
    if came.shape[0] == 2:
        first = (first + came[0].astype(F32)).astype(BF16)
        second = (second + came[1].astype(F32)).astype(BF16)
    else:
        first = (first + came[0, :, :width].astype(F32)).astype(BF16)
        second = (second + came[0, :, width:].astype(F32)).astype(BF16)

    def store(ref, rows):
        if ref.shape[0] == 2:
            ref[0] = first[rows]
            ref[1] = second[rows]
        else:
            ref[0, :, :width] = first[rows]
            ref[0, :, width:] = second[rows]

    for k in range(4):

        @pl.when(step == k)
        def _(k=k):
            if k == 0:
                store(outs[0], slice(0, 256))
            else:
                store(outs[2 * k - 1], slice(0, 128))
                store(outs[2 * k], slice(128, 256))


def fold_call(forth, back, normed_t, grad_t, came, sizes, estimate):
    whole = lambda i: (0, 0)
    lead, _, wide = came.shape
    own = lambda i: (4 + i, 0)
    return pl.pallas_call(
        fold_kernel,
        grid=(4,),
        in_specs=[
            pl.BlockSpec(forth.shape, whole, pipeline_mode=ONCE),
            pl.BlockSpec(back.shape, whole, pipeline_mode=ONCE),
            pl.BlockSpec((256, TOKENS), own),
            pl.BlockSpec((256, TOKENS), own),
            pl.BlockSpec((lead, 256, wide), lambda i: (0, i, 0)),
        ],
        out_specs=[pl.BlockSpec((lead, n, wide), lambda i: (0, 0, 0)) for n in sizes],
        out_shape=[shape((lead, n, wide), BF16) for n in sizes],
        compiler_params=params(63),
        cost_estimate=cost(estimate),
        name="fold",
    )(forth, back, normed_t, grad_t, came)


def mlp_kernel(normed, grad, normed_t, grad_t, up, down, bias, weight_grad, branch, back, bias_grad, ups, downs, actives, grads):
    step = pl.program_id(0)

    @pl.when(step < 4)
    def _():
        hidden = dot(normed[...], up[...]) + bias[...]
        square = hidden * hidden
        slope = 0.7978845608028654
        turn = jnp.tanh(slope * (hidden + 0.044715 * (square * hidden)))
        half = 0.5 * (1.0 + turn)
        derivative = half + 0.5 * hidden * (1.0 - turn * turn) * (slope * (1.0 + 0.134145 * square))
        grad_hidden = (dot(grad[...], down[...]) * derivative).astype(BF16)
        columns = lane_block(step, 256)
        actives[:, columns] = (hidden * half).astype(BF16)
        grads[:, columns] = grad_hidden
        ups[:, columns] = up[...]
        downs[:, columns] = down[...]
        bias_grad[...] = jnp.sum(grad_hidden.astype(F32), axis=0, keepdims=True)

    @pl.when(step >= 4)
    def _():
        rows = lane_block(step - 4, 512)
        branch[...] = dot_nt(actives[...], downs[rows, :]).astype(BF16)
        back[...] = dot_nt(grads[...], ups[rows, :]).astype(BF16)
        weight_grad[0] = dot(normed_t[...], grads[...]).astype(BF16)
        weight_grad[1] = dot(grad_t[...], actives[...]).astype(BF16)


def mlp_call(normed, grad, normed_t, grad_t, weight, base, bias):
    whole = lambda i: (0, 0)
    early = lambda i: jnp.minimum(i, 3)
    late = lambda i: jnp.maximum(i - 4, 0)
    return pl.pallas_call(
        mlp_kernel,
        grid=(8,),
        in_specs=[
            pl.BlockSpec((TOKENS, WIDTH), whole, pipeline_mode=ONCE),
            pl.BlockSpec((TOKENS, WIDTH), whole, pipeline_mode=ONCE),
            pl.BlockSpec((512, TOKENS), lambda i: (late(i), 0)),
            pl.BlockSpec((512, TOKENS), lambda i: (late(i), 0)),
            pl.BlockSpec((WIDTH, 256), lambda i: (0, base + early(i))),
            pl.BlockSpec((WIDTH, 256), lambda i: (0, base + 4 + early(i))),
            pl.BlockSpec((1, 256), lambda i: (0, early(i))),
        ],
        out_specs=[
            pl.BlockSpec((2, 512, 1024), lambda i: (0, late(i), 0)),
            pl.BlockSpec((TOKENS, 512), lambda i: (0, late(i))),
            pl.BlockSpec((TOKENS, 512), lambda i: (0, late(i))),
            pl.BlockSpec((1, 256), lambda i: (0, early(i))),
        ],
        out_shape=[
            shape((2, WIDTH, 1024), BF16),
            shape((TOKENS, WIDTH), BF16),
            shape((TOKENS, WIDTH), BF16),
            shape((1, 1024), F32),
        ],
        scratch_shapes=[
            pltpu.VMEM((WIDTH, 1024), BF16),
            pltpu.VMEM((WIDTH, 1024), BF16),
            pltpu.VMEM((TOKENS, 1024), BF16),
            pltpu.VMEM((TOKENS, 1024), BF16),
        ],
        compiler_params=params(63),
        cost_estimate=cost(12),
        name="mlp",
    )(normed, grad, normed_t, grad_t, weight, weight, bias)


def collect_kernel(where, q0, q1, q2, q3, normed_t, grad_t, grads, contexts, bias_grad, other):
    for k, ref in enumerate((q0, q1, q2, q3)):
        group = lax.rem(where[1] + k, 4)
        grads[:, lane_block(group, 384)] = ref[:, :384]
        contexts[:, lane_block(group, 128)] = ref[:, 384:]
    bias_grad[...] = jnp.sum(grads[...].astype(F32), axis=0, keepdims=True)
    other[0, :, :1536] = dot(normed_t[...], grads[...]).astype(BF16)
    other[0, :, 1536:] = dot(grad_t[...], contexts[...]).astype(BF16)


def collect_call(where, pieces, normed_t, grad_t):
    return pl.pallas_call(
        collect_kernel,
        grid=(1,),
        in_specs=[SMEM_SPEC] + [pl.BlockSpec((TOKENS, 512), lambda i: (0, 0))] * 4
        + [pl.BlockSpec((1024, TOKENS), lambda i: (0, 0))] * 2,
        out_specs=[VMEM_SPEC] * 4,
        out_shape=[
            shape((TOKENS, 1536), BF16),
            shape((TOKENS, 512), BF16),
            shape((1, 1536), F32),
            shape((1, 1024, WIDTH), BF16),
        ],
        compiler_params=params(63),
        cost_estimate=cost(4),
        name="collect",
    )(where, *pieces, normed_t, grad_t)


def mix_kernel(context, w_dense, b0, b1, out):
    total = dot_nt(context[...], w_dense[...]) + b0[...].astype(F32) + b1[...].astype(F32)
    out[...] = total.astype(BF16)


def mix_call(context, weight, branch0, branch1):
    column = pl.BlockSpec((TOKENS, 512), lambda i: (0, i))
    return pl.pallas_call(
        mix_kernel,
        grid=(4,),
        in_specs=[
            pl.BlockSpec((TOKENS, 512), lambda i: (0, 0), pipeline_mode=ONCE),
            pl.BlockSpec((512, 512), lambda i: (i, 3)),
            column,
            column,
        ],
        out_specs=column,
        out_shape=shape((TOKENS, WIDTH), BF16),
        compiler_params=params(63),
        cost_estimate=cost(6),
        name="mix",
    )(context, weight, branch0, branch1)


def close_kernel(
    where, grad_qkv, w_qkv, mix, g0, g1, rows, stats, gain, w0, w1, w2, w3, tails, raws, standards, branches, sums
):
    step = pl.program_id(0)
    lane = lax.broadcasted_iota(jnp.int32, (TOKENS, 128), 1)

    @pl.when(step == 0)
    def _():
        sums[...] = jnp.zeros((TOKENS, 128), F32)

    @pl.when(step < 4)
    def _():
        branches[step] = mix[...]
        raw = dot_nt(grad_qkv[...], w_qkv[...]) + g0[...].astype(F32) + g1[...].astype(F32)
        scaled = raw * gain[step]
        raws[step] = scaled
        standard = (rows[...].astype(F32) - stats[:, 0:1]) * stats[:, 1:2]
        standards[step] = standard
        first = jnp.sum(scaled, axis=1, keepdims=True)
        second = jnp.sum(scaled * standard, axis=1, keepdims=True)
        sums[...] += jnp.where(lane == 0, first, second) * (1.0 / WIDTH)
        row = lax.broadcasted_iota(jnp.int32, (8, 512), 0)
        gain_sum = jnp.sum(raw * standard, axis=0, keepdims=True)
        tails[...] = jnp.where(row == 0, gain_sum, jnp.sum(raw, axis=0, keepdims=True))

    for k, out in enumerate((w0, w1, w2, w3)):

        @pl.when(step == 4 + k)
        def _(out=out, k=k):
            block = lax.rem(where[0] + k, 4)
            whole = raws[block] - sums[:, 0:1] - standards[block] * sums[:, 1:2]
            out[0:512, :] = (stats[:, 1:2] * whole).astype(BF16)
            out[512:1024, :] = branches[block]


def close_call(where, grad_qkv, weight, mix, backs, rows, stats, gain):
    whole = lambda i: (0, 0)
    row = lambda i: jnp.minimum(i, 3)
    column = pl.BlockSpec((TOKENS, 512), lambda i: (0, row(i)))
    sizes = (1024,) * 4
    return pl.pallas_call(
        close_kernel,
        grid=(8,),
        in_specs=[
            SMEM_SPEC,
            pl.BlockSpec((TOKENS, 1536), whole, pipeline_mode=ONCE),
            pl.BlockSpec((512, 1536), lambda i: (row(i), 0)),
        ]
        + [column] * 4
        + [
            pl.BlockSpec((TOKENS, 128), whole, pipeline_mode=ONCE),
            pl.BlockSpec((4, 1, 512), lambda i: (0, 0, 0), pipeline_mode=ONCE),
        ],
        out_specs=[pl.BlockSpec((n, 512), whole) for n in sizes] + [pl.BlockSpec((8, 512), lambda i: (0, row(i)))],
        out_shape=[shape((n, 512), BF16) for n in sizes] + [shape((8, WIDTH), F32)],
        scratch_shapes=[
            pltpu.VMEM((4, TOKENS, 512), F32),
            pltpu.VMEM((4, TOKENS, 512), F32),
            pltpu.VMEM((4, TOKENS, 512), BF16),
            pltpu.VMEM((TOKENS, 128), F32),
        ],
        compiler_params=params(63),
        cost_estimate=cost(15),
        name="close",
    )(where, grad_qkv, weight, mix, *backs, rows, stats, gain)


def rotary_tables(segments):
    position = jnp.arange(LENGTH, dtype=jnp.int32)[None, :]
    one = jnp.sum((segments < 1).astype(jnp.int32), axis=1, keepdims=True)
    two = jnp.sum((segments < 2).astype(jnp.int32), axis=1, keepdims=True)
    low = jnp.where(segments == 0, 0, jnp.where(segments == 1, one, two))
    exponent = jnp.arange(ROT // 2, dtype=F32) * (2.0 / ROT)
    frequency = jnp.power(10000.0, -exponent)
    angles = (position - low).astype(F32)[:, None, :] * frequency[None, :, None]
    return jnp.broadcast_to(low[:, None, :], (low.shape[0], 8, LENGTH)), jnp.cos(angles), jnp.sin(angles)


def add(*arrays):
    total = arrays[0].astype(F32)
    for array in arrays[1:]:
        total = total + array.astype(F32)
    return total


def shift_y(array, step):
    return lax.ppermute(array, "fsdp", [(i, (i + 2 * step) % 8) for i in range(8)])


def swap_core(array):
    return lax.ppermute(array, "fsdp", [(i, i ^ 1) for i in range(8)])


def after(value, *others):
    return lax.optimization_barrier((value,) + others)[0]


def sum_x(parts):
    return [add(*(p[:, 64 * k : 64 * k + 64] for p in parts)).astype(BF16) for k in range(4)]


def local(tokens, segments, gain, shift_, w_qkv, b_qkv, w_dense, b_dense, w_fc1, b_fc1, w_fc2, b_fc2, cotangent):
    x = lax.axis_index("ctx").astype(jnp.int32)
    z = lax.axis_index("tp").astype(jnp.int32)
    f = lax.axis_index("fsdp").astype(jnp.int32)
    seqs = tokens.shape[0]
    mine = tokens.reshape(TOKENS, 512)
    grad = cotangent.reshape(TOKENS, 512)
    where = jnp.stack([z, x, f // 2, f % 2])

    early = pick_call(where[1:2], w_qkv, w_dense, w_fc1, w_fc2)
    early, mine, grad, gain = lax.optimization_barrier((early, mine, grad, gain))
    wa = lax.all_gather(early, ("fsdp", "ctx"), axis=0, tiled=True)
    affine = jnp.stack(split_three(gain) + split_three(shift_) + [jnp.zeros((512,), BF16)] * 10)
    send = jnp.concatenate([mine, affine], axis=0)

    t1, t3 = shift(send, "tp", 1), shift(send, "tp", 3)
    g1, g3 = shift(grad, "tp", 1), shift(grad, "tp", 3)
    t2 = shift(t1, "tp", 1)
    g2 = shift(g3, "tp", 3)
    normed, normed_n, normed_s, rows, stats, gain_full = norm_call(where, [send, t1, t2, t3])
    grad_full, grad_n, grad_s = join_call(where, [grad, g1, g2, g3])

    late = jnp.concatenate([w_fc1[:, 1024:], w_fc2[:, 1024:]], axis=1)
    bias = b_qkv.reshape(1, 1536)
    bias_ff = [b_fc1[:1024].reshape(1, 1024), b_fc1[1024:].reshape(1, 1024)]
    tables = rotary_tables(segments)
    normed, grad_full, late, tables, bias, bias_ff = lax.optimization_barrier(
        (normed, grad_full, late, tables, bias, bias_ff)
    )
    low, cosine, sine = tables
    late, wa, normed = lax.optimization_barrier((late, wa, normed))
    wb = lax.all_gather(late, "fsdp", axis=0, tiled=True)

    kept, *sent = project_call(where, normed, grad_full, wa, bias)
    arrived = [shift(a, "ctx", k + 1) for k, a in enumerate(sent)]
    ff0 = mlp_call(after(normed, kept), grad_full, normed_n, grad_n, wa, 8, bias_ff[0])
    *arrived, f0 = lax.optimization_barrier((kept, *arrived, ff0[0]))
    f0 = lax.psum_scatter(f0, "fsdp", scatter_dimension=1, tiled=True)
    done = attention_call(where[1:2], [a.reshape(seqs, ROWS, 512) for a in arrived], low, cosine, sine)
    done = [a.reshape(TOKENS, 512) for a in done]
    returned = [done[0]] + [shift(a, "ctx", 4 - k) for k, a in enumerate(done) if k > 0]
    ff1 = mlp_call(after(normed, done[0]), grad_full, normed_n, grad_n, wb, 0, bias_ff[1])
    *returned, f1 = lax.optimization_barrier((*returned, ff1[0]))
    f1 = lax.psum_scatter(f1, "fsdp", scatter_dimension=1, tiled=True)
    grad_qkv, context, bias_grad_a, other_a = collect_call(where, returned, normed_s, grad_s)
    came_a = swap_core(other_a)
    mix = mix_call(after(context, other_a), wa, ff0[1], ff1[1])
    a0, a1t, a1b, a2t, a2b, a3t, a3b = fold_call(
        after(context, mix), grad_qkv, normed_s, grad_s, came_a, (256,) + (128,) * 6, 20
    )
    up, down = shift(a2t, "ctx", 1), shift(a2b, "ctx", 3)
    *w, tails = close_call(
        where[0:1], after(grad_qkv, a0), wa, mix, [ff0[2], ff1[2]], rows, stats, gain_full
    )
    up, down, w, tails = lax.optimization_barrier((up, down, w, tails))
    w1, w3 = shift(w[1], "tp", 1), shift(w[3], "tp", 3)
    small = jnp.concatenate(
        [tails[0:2].reshape(4096), jnp.sum(grad.astype(F32), axis=0), bias_grad_a[0], ff0[3][0], ff1[3][0]]
    )
    small = small + swap_core(small)
    up, down, small = lax.optimization_barrier((up, down, small))
    up = shift(jnp.concatenate([add(a1t, up).astype(BF16), a1b], axis=1), "ctx", 1)
    down = shift(jnp.concatenate([a3t, add(a3b, down).astype(BF16)], axis=1), "ctx", 3)
    small = small + lax.ppermute(small, "fsdp", [(i, i ^ 2) for i in range(8)])
    small = small + lax.ppermute(small, "fsdp", [(i, i ^ 4) for i in range(8)])
    both, small = small[:4096], small[4096:]
    both = both + lax.ppermute(both, "tp", [(i, i ^ 1) for i in range(4)])
    both = both + lax.ppermute(both, "tp", [(i, i ^ 2) for i in range(4)])
    small = jnp.concatenate([both, small])
    small = small + lax.ppermute(small, "ctx", [(i, i ^ 1) for i in range(4)])
    up, down, w1, w3, small, w2, f0, f1 = lax.optimization_barrier((up, down, w1, w3, small, w[2], f0, f1))
    f01 = lax.psum_scatter(jnp.concatenate([f0, f1]), "ctx", scatter_dimension=1, tiled=True)
    w2 = shift(w2, "tp", 2)
    ja = sum_x([a0, up, down])
    ya = [shift_y(ja[k], k) for k in (1, 2, 3)]
    small = small + lax.ppermute(small, "ctx", [(i, i ^ 2) for i in range(4)])
    ya, small, w2, f01 = lax.optimization_barrier((ya, small, w2, f01))
    both, small = small[:4096], small[4096:]
    total = add(w[0], w1, w2, w3)
    f01 = f01.astype(F32)
    grad_tokens = (grad.astype(F32) + total[:512]).reshape(tokens.shape)
    mixed = (mine.astype(F32) + total[512:] + b_dense + b_fc2).astype(BF16).reshape(tokens.shape)

    ga = add(ja[0], *ya)[0]
    grad_w_fc1 = jnp.concatenate([f01[0], f01[2]], axis=1)
    grad_w_fc2 = jnp.concatenate([f01[1], f01[3]], axis=1)
    both = lax.dynamic_index_in_dim(both.reshape(2, 4, 512), z, 1, keepdims=False)
    grad_b_out = small[:512]
    return (
        mixed,
        grad_tokens,
        both[0],
        both[1],
        ga[:, :1536],
        small[512:2048],
        ga[:, 1536:],
        grad_b_out,
        grad_w_fc1,
        small[2048:],
        grad_w_fc2,
        grad_b_out,
    )


def solution(mesh):
    token = P("fsdp", "ctx", "tp")
    weight = P("fsdp", "tp")
    weight_grad = P(("fsdp", "ctx"), "tp")
    vector = P("tp")
    return jax.shard_map(
        local,
        mesh=mesh,
        in_specs=(
            token, P("fsdp", None), vector, vector, weight, vector, weight, vector, weight, vector, weight, vector, token,
        ),
        out_specs=(
            token, token, vector, vector, weight_grad, vector, weight_grad, vector, weight_grad, vector, weight_grad, vector,
        ),
        check_vma=False,
    )
```
